32 devices in a mesh: seq: 16 (over z, x, core), chan: 2 (over y).
Axes of the slice: x: 2, y: 2, z: 4, core: 2. Of those that a mesh axis runs over, the one named last changes fastest.
Arguments:
- signal: bfloat16 [2, 8192, 128], P('chan', 'seq'), may hold values from -6 to 6
- cotangent: bfloat16 [2, 8192, 128], P('chan', 'seq'), may hold values from -6 to 6
- band_freq: int32 [16], replicated, may hold values from 1 to 2047
- w_embed: float32 [32, 64], replicated, may hold values from -2 to 2
- b_embed: float32 [64], replicated, may hold values from -3.140625 to 3.140625
- w_out: float32 [64, 128], P(None, 'chan'), may hold values from -0.75 to 0.75
- decay: float32 [128], P('chan'), may hold values from 0.25 to 16, as said below
Outputs:
- conv_out: bfloat16 [2, 8192, 128], P('chan', 'seq')
- d_signal: bfloat16 [2, 8192, 128], P('chan', 'seq')
- grad_embed: float32 [32, 64], replicated
- grad_bias: float32 [64], replicated
- grad_out: float32 [64, 128], P(None, 'chan')
The draws below stay inside these ranges and needn't reach their ends.
Inputs may be any that keep to these rules, and one draw needn't show every extreme that they name: decay rates are positive.
All inputs are finite; a program needn't handle non-finite values.
Results may differ from the reference program's by a relative error of at most 0.007.
Values may be sent and summed in bfloat16 or wider, within the bound.
A program may use at most 192 MiB of HBM per device.

```python
import math
import jax
import jax.numpy as jnp
from jax import lax

CG = 64
E = 32
F = 64
L = 16384
CHANNELS = 128
N_CHAN = 2


def draw_decay(key, part):
    rate_key = jax.random.fold_in(key, 0)
    low_log = math.log(0.5)
    high_log = math.log(12.0)
    rates = jnp.exp(jax.random.uniform(rate_key, (CHANNELS,), jnp.float32, low_log, high_log))
    rates = jnp.clip(rates, 0.25, 16.0)
    return rates.astype(jnp.float32)


def with_ends(values, own_key, low, largest):
    index_at = [jax.random.randint(jax.random.fold_in(own_key, axis), (), 0, length) for axis, length in enumerate(values.shape)]
    widest = values.shape.index(max(values.shape))
    neighbour = index_at[:widest] + [(index_at[widest] + 1) % values.shape[widest]] + index_at[widest + 1:]
    return values.at[tuple(index_at)].set(low).at[tuple(neighbour)].set(largest)


def shard_levels(own_key, shape, shards, smallest, top_value):
    factor_of, own = 1.0, jax.random.fold_in(own_key, 6)
    for dim, shards_of in shards:
        draws = jnp.exp(jax.random.uniform(jax.random.fold_in(own, dim), (shards_of,), jnp.float32, smallest / len(shards), top_value / len(shards)))
        factor_of = factor_of * jnp.repeat(draws, shape[dim] // shards_of).reshape([-1 if axis == dim else 1 for axis in range(len(shape))])
    return factor_of


def gaussian(own_key, shape, width, bound, cuts=(), kind=jnp.bfloat16):
    entries = width * jax.random.normal(own_key, shape, jnp.float32)
    if cuts:
        entries = entries * shard_levels(own_key, shape, cuts, -0.22, 0.18)
    return jnp.clip(entries, -bound, bound).astype(kind)


def setup_inputs(seed: int = 0) -> dict:
    arg_keys = jax.random.split(jax.random.key(seed), 8)
    signal = gaussian(arg_keys[0], (N_CHAN, L // 2, 2 * CG), 1.0, 6.0, ((0, 2), (1, 16)))
    cotangent = gaussian(arg_keys[1], (N_CHAN, L // 2, 2 * CG), 1.0, 6.0, ((0, 2), (1, 16)))
    band_freq = with_ends(jax.random.randint(arg_keys[2], (E // 2,), 1, L // 8), jax.random.fold_in(arg_keys[2], 1), 1, (L // 8) - 1).astype(jnp.int32)
    w_embed = gaussian(arg_keys[3], (E, F), (E // 4) ** -0.5, 2.0, (), jnp.float32)
    b_embed = jnp.clip(jax.random.uniform(arg_keys[4], (F,), jnp.float32, -3.140625, 3.140625), -3.140625, 3.140625)
    w_out = gaussian(arg_keys[5], (F, CHANNELS), F ** -0.5, 0.75, ((1, 2),), jnp.float32)
    decay = draw_decay(jax.random.fold_in(arg_keys[7], 71), 0)
    return {"signal": signal, "cotangent": cotangent, "band_freq": band_freq, "w_embed": w_embed, "b_embed": b_embed, "w_out": w_out, "decay": decay}


exact_mode = lax.Precision.HIGHEST

def mat_dot(lhs_mat, rhs_mat):
    return jnp.dot(lhs_mat, rhs_mat, preferred_element_type=jnp.float32, precision=exact_mode)

def band_phase(band_freq, places, seq_total):
    upper_part = places // 1024
    lower_part = places % 1024
    partial_turn = upper_part[:, None] * band_freq[None, :] % seq_total
    wrapped = (partial_turn * 1024 + lower_part[:, None] * band_freq[None, :]) % seq_total
    return wrapped.astype(jnp.float32) * (2.0 * math.pi / seq_total)

def filter_parts(places, band_freq, w_embed, b_embed, w_out, decay, seq_total):
    phases = band_phase(band_freq, places, seq_total)
    features = jnp.concatenate([jnp.cos(phases), jnp.sin(phases)], axis=1)
    preact = mat_dot(features, w_embed) + b_embed[None, :]
    hidden = jnp.sin(preact)
    fraction = places.astype(jnp.float32) / seq_total
    envelope = jnp.exp(-decay[None, :] * fraction[:, None]) * jnp.sqrt((1.0 + decay) / seq_total)[None, :]
    taps = mat_dot(hidden, w_out) * envelope
    return (features, preact, hidden, taps, envelope)

def to_rows(blocks):
    return blocks.reshape(N_CHAN, L, CG).transpose(1, 0, 2).reshape(L, N_CHAN * CG)

def to_blocks(rows_data):
    return rows_data.reshape(L, N_CHAN, CG).transpose(1, 0, 2).reshape(N_CHAN, L // 2, 2 * CG)

def reference(signal, cotangent, band_freq, w_embed, b_embed, w_out, decay):
    fft_size = 2 * L
    places = jnp.arange(L, dtype=jnp.int32)
    features, preact, hidden, taps, envelope = filter_parts(places, band_freq, w_embed, b_embed, w_out, decay, L)
    source = to_rows(signal).astype(jnp.float32)
    upstream = to_rows(cotangent).astype(jnp.float32)
    spec_src = jnp.fft.rfft(source, n=fft_size, axis=0)
    spec_up = jnp.fft.rfft(upstream, n=fft_size, axis=0)
    spec_taps = jnp.fft.rfft(taps, n=fft_size, axis=0)
    conv_rows = jnp.fft.irfft(spec_src * spec_taps, n=fft_size, axis=0)[:L].astype(jnp.bfloat16)
    dsig_rows = jnp.fft.irfft(spec_up * jnp.conj(spec_taps), n=fft_size, axis=0)[:L].astype(jnp.bfloat16)
    d_taps = jnp.fft.irfft(spec_up * jnp.conj(spec_src), n=fft_size, axis=0)[:L]
    d_raw = d_taps * envelope
    d_preact = mat_dot(d_raw, w_out.T) * jnp.cos(preact)
    norm_scale = 1.0 / math.sqrt(L)
    grad_out = mat_dot(hidden.T, d_raw) * norm_scale
    grad_embed = mat_dot(features.T, d_preact) * norm_scale
    grad_bias = lax.optimization_barrier(jnp.sum(d_preact, axis=0)) * norm_scale
    return (to_blocks(conv_rows), to_blocks(dsig_rows), grad_embed, grad_bias, grad_out)
```

```python
import functools
import math

import jax
import jax.numpy as jnp
import numpy as np
from jax import lax
from jax.experimental import pallas as pl
from jax.experimental.pallas import tpu as pltpu
from jax.sharding import PartitionSpec as P

exact_mode = lax.Precision.HIGHEST


def mat_dot(lhs_mat, rhs_mat):
    return jnp.dot(lhs_mat, rhs_mat, preferred_element_type=jnp.float32, precision=exact_mode)


def side_dot(table, values):
    return jnp.einsum(
        "db,cbm->cdm", table, values, preferred_element_type=jnp.float32, precision=exact_mode
    )


def inner_dot(table, values):
    return jnp.einsum(
        "eb,cdbh->cdeh", table, values, preferred_element_type=jnp.float32, precision=exact_mode
    )


def band_phase(band_freq, places, seq_total):
    upper_part = places // 1024
    lower_part = places % 1024
    partial_turn = upper_part[:, None] * band_freq[None, :] % seq_total
    wrapped = (partial_turn * 1024 + lower_part[:, None] * band_freq[None, :]) % seq_total
    return wrapped.astype(jnp.float32) * (2.0 * math.pi / seq_total)


def filter_parts(places, band_freq, w_embed, b_embed, w_out, decay, seq_total):
    phases = band_phase(band_freq, places, seq_total)
    features = jnp.concatenate([jnp.cos(phases), jnp.sin(phases)], axis=1)
    preact = mat_dot(features, w_embed) + b_embed[None, :]
    hidden = jnp.sin(preact)
    fraction = places.astype(jnp.float32) / seq_total
    envelope = (
        jnp.exp(-decay[None, :] * fraction[:, None]) * jnp.sqrt((1.0 + decay) / seq_total)[None, :]
    )
    taps = mat_dot(hidden, w_out) * envelope
    return (features, preact, hidden, taps, envelope)


def angle_table(rows_idx, cols_idx, modulus):
    wrapped = rows_idx[:, None] * cols_idx[None, :] % modulus
    angles = wrapped.astype(jnp.float32) * (2.0 * math.pi / modulus)
    return (jnp.cos(angles), jnp.sin(angles))


def local_any(signal, cotangent, band_freq, w_embed, b_embed, w_out, decay):
    devices = lax.axis_size("seq")
    rank_seq = lax.axis_index("seq")
    seg_len = signal.shape[1] * 2
    channels = signal.shape[2] // 2
    block_w = seg_len // devices
    rows_all = 2 * devices
    seq_total = seg_len * devices
    fft_size = 2 * seq_total
    inv_scale = 1.0 / fft_size
    radix_one = max(
        (divisor for divisor in range(1, math.isqrt(seg_len) + 1) if seg_len % divisor == 0)
    )
    radix_two = seg_len // radix_one
    row_ids = jnp.arange(rows_all, dtype=jnp.int32)
    src_ids = jnp.arange(devices, dtype=jnp.int32)
    col_glob = rank_seq * block_w + jnp.arange(block_w, dtype=jnp.int32)
    seg_ids = jnp.arange(seg_len, dtype=jnp.int32)
    one_ids = jnp.arange(radix_one, dtype=jnp.int32)
    two_ids = jnp.arange(radix_two, dtype=jnp.int32)
    pair_ids = lax.dynamic_slice_in_dim(row_ids, 2 * rank_seq, 2)
    outer_cos, outer_sin = angle_table(row_ids, src_ids, rows_all)
    entry_cos, entry_sin = angle_table(row_ids, col_glob, fft_size)
    first_cos, first_sin = angle_table(one_ids, one_ids, radix_one)
    second_cos, second_sin = angle_table(two_ids, two_ids, radix_two)
    inner_cos, inner_sin = angle_table(one_ids, two_ids, seg_len)
    exit_cos, exit_sin = angle_table(pair_ids, seg_ids, fft_size)
    inner_c = inner_cos[None, :, :, None]
    inner_s = inner_sin[None, :, :, None]

    def twist_stack(real_a, imag_a):
        real_a = real_a.reshape(rows_all, block_w, channels)
        imag_a = imag_a.reshape(rows_all, block_w, channels)
        twist_c = entry_cos[:, :, None]
        twist_s = entry_sin[:, :, None]
        real_b = real_a * twist_c + imag_a * twist_s
        imag_b = imag_a * twist_c - real_a * twist_s
        return jnp.stack([real_b, imag_b]).reshape(2, rows_all, block_w * channels)

    def column_pass(cols_data):
        return twist_stack(mat_dot(outer_cos, cols_data), -mat_dot(outer_sin, cols_data))

    def local_forward(stacked):
        grid = stacked.reshape(2, 2, radix_one, radix_two * channels)
        part_r = side_dot(first_cos, grid[0]) + side_dot(first_sin, grid[1])
        part_i = side_dot(first_cos, grid[1]) - side_dot(first_sin, grid[0])
        part_r = part_r.reshape(2, radix_one, radix_two, channels)
        part_i = part_i.reshape(2, radix_one, radix_two, channels)
        turn_r = part_r * inner_c + part_i * inner_s
        turn_i = part_i * inner_c - part_r * inner_s
        spec_r = inner_dot(second_cos, turn_r) + inner_dot(second_sin, turn_i)
        spec_i = inner_dot(second_cos, turn_i) - inner_dot(second_sin, turn_r)
        return (spec_r, spec_i)

    def local_inverse(spec_r, spec_i):
        back_r = inner_dot(second_cos, spec_r) - inner_dot(second_sin, spec_i)
        back_i = inner_dot(second_cos, spec_i) + inner_dot(second_sin, spec_r)
        turn_r = (back_r * inner_c - back_i * inner_s).reshape(2, radix_one, radix_two * channels)
        turn_i = (back_r * inner_s + back_i * inner_c).reshape(2, radix_one, radix_two * channels)
        time_r = (side_dot(first_cos, turn_r) - side_dot(first_sin, turn_i)).reshape(
            2, seg_len, channels
        )
        time_i = (side_dot(first_cos, turn_i) + side_dot(first_sin, turn_r)).reshape(
            2, seg_len, channels
        )
        twist_c = exit_cos[:, :, None]
        twist_s = exit_sin[:, :, None]
        final_r = time_r * twist_c - time_i * twist_s
        final_i = time_r * twist_s + time_i * twist_c
        return jnp.stack([final_r, final_i]).reshape(2, 2, seg_len * channels)

    def real_rows(gathered):
        return mat_dot(outer_cos.T, gathered[0]) - mat_dot(outer_sin.T, gathered[1])

    sig_cols, cot_cols = (
        lax.all_to_all(
            signal.reshape(devices, block_w * channels),
            "seq",
            split_axis=0,
            concat_axis=0,
            tiled=True,
        ),
        lax.all_to_all(
            cotangent.reshape(devices, block_w * channels),
            "seq",
            split_axis=0,
            concat_axis=0,
            tiled=True,
        ),
    )
    places = rank_seq * seg_len + seg_ids
    features, preact, hidden, taps, envelope = filter_parts(
        places, band_freq, w_embed, b_embed, w_out, decay, seq_total
    )
    tap_cols = lax.all_to_all(
        taps.reshape(devices, block_w * channels), "seq", split_axis=0, concat_axis=0, tiled=True
    )
    spec_sig, spec_cot, spec_tap = (
        lax.all_to_all(
            column_pass(sig_cols.astype(jnp.float32)),
            "seq",
            split_axis=1,
            concat_axis=2,
            tiled=True,
        ),
        lax.all_to_all(
            column_pass(cot_cols.astype(jnp.float32)),
            "seq",
            split_axis=1,
            concat_axis=2,
            tiled=True,
        ),
        lax.all_to_all(column_pass(tap_cols), "seq", split_axis=1, concat_axis=2, tiled=True),
    )
    sig_r, sig_i = local_forward(spec_sig)
    cot_r, cot_i = local_forward(spec_cot)
    tap_r, tap_i = local_forward(spec_tap)
    prod_r = sig_r * tap_r - sig_i * tap_i
    prod_i = sig_r * tap_i + sig_i * tap_r
    grad_r = cot_r * tap_r + cot_i * tap_i
    grad_i = cot_i * tap_r - cot_r * tap_i
    corr_r = cot_r * sig_r + cot_i * sig_i
    corr_i = cot_i * sig_r - cot_r * sig_i
    prod_back, grad_back, corr_back = (
        lax.all_to_all(
            local_inverse(prod_r, prod_i), "seq", split_axis=2, concat_axis=1, tiled=True
        ),
        lax.all_to_all(
            local_inverse(grad_r, grad_i), "seq", split_axis=2, concat_axis=1, tiled=True
        ),
        lax.all_to_all(
            local_inverse(corr_r, corr_i), "seq", split_axis=2, concat_axis=1, tiled=True
        ),
    )
    out_cols = real_rows(prod_back)
    dsig_cols = real_rows(grad_back)
    dtap_cols = real_rows(corr_back) * inv_scale
    out_rows, dsig_rows = (
        lax.all_to_all(
            (out_cols * inv_scale).astype(jnp.bfloat16),
            "seq",
            split_axis=0,
            concat_axis=0,
            tiled=True,
        ),
        lax.all_to_all(
            (dsig_cols * inv_scale).astype(jnp.bfloat16),
            "seq",
            split_axis=0,
            concat_axis=0,
            tiled=True,
        ),
    )
    conv_out = out_rows.reshape(1, seg_len // 2, 2 * channels)
    d_signal = dsig_rows.reshape(1, seg_len // 2, 2 * channels)
    d_taps = (
        lax.all_to_all(
            dtap_cols.astype(jnp.bfloat16), "seq", split_axis=0, concat_axis=0, tiled=True
        )
        .astype(dtap_cols.dtype)
        .reshape(seg_len, channels)
    )
    d_raw = d_taps * envelope
    d_preact = mat_dot(d_raw, w_out.T) * jnp.cos(preact)
    out_part = mat_dot(hidden.T, d_raw)
    embed_part = mat_dot(features.T, d_preact)
    bias_part = jnp.sum(d_preact, axis=0)
    out_sum, embed_sum, bias_sum = lax.psum((out_part, embed_part, bias_part), "seq")
    embed_all, bias_all = lax.psum((embed_sum, bias_sum), "chan")
    norm_scale = 1.0 / math.sqrt(seq_total)
    return (conv_out, d_signal, embed_all * norm_scale, bias_all * norm_scale, out_sum * norm_scale)


WIDE = 256
HALF = 128


def split_np(table):
    high = table.astype(jnp.bfloat16)
    low = (table - high.astype(np.float64)).astype(jnp.bfloat16)
    return np.stack([high, low])


def const_tables(devices, own, segs):
    blocks = devices * segs
    total = 2 * blocks * WIDE
    eye = np.eye(own)
    half_f = np.arange(blocks) + 0.5
    alpha = 2 * np.pi * half_f[:, None] * np.arange(blocks)[None, :] / (2 * blocks)
    outer = np.concatenate([np.kron(np.cos(alpha), eye), np.kron(-np.sin(alpha), eye)])
    lane = np.arange(WIDE)
    places = 2 * (lane % HALF) + lane // HALF
    theta = np.repeat(2 * np.pi * half_f[:, None] * places[None, :] / total, own, axis=0)
    twist = np.stack([np.cos(theta), np.sin(theta)]).astype(np.float32)
    phi = 2 * np.pi * (places[:, None] * np.arange(WIDE)[None, :] % WIDE) / WIDE
    inner = np.block([[np.cos(phi), -np.sin(phi)], [np.sin(phi), np.cos(phi)]])
    chans = devices * own
    pick = np.zeros((2, devices, segs, own, segs, 2, chans), np.float32)
    for h in range(2):
        for r in range(devices):
            for q in range(segs):
                for k in range(own):
                    pick[h, r, q, k, q, h, r * own + k] = 1.0
    pick = pick.reshape(2, devices * segs * own, segs * 2 * chans).astype(jnp.bfloat16)
    return split_np(outer), split_np(inner), twist, pick


def dot_nn(lhs, rhs):
    return lax.dot_general(lhs, rhs, (((1,), (0,)), ((), ())), preferred_element_type=jnp.float32)


def dot_nt(lhs, rhs):
    return lax.dot_general(lhs, rhs, (((1,), (1,)), ((), ())), preferred_element_type=jnp.float32)


def dot_tn(lhs, rhs):
    return lax.dot_general(lhs, rhs, (((0,), (0,)), ((), ())), preferred_element_type=jnp.float32)


def sin_cos(quarter):
    whole = jnp.round(quarter)
    rest = quarter - whole
    sq = rest * rest
    sin_p = rest * (1.5707963268 + sq * (-0.6459640975 + sq * (0.0796926262 + sq * (-0.0046817541 + sq * 0.00016044118))))
    cos_p = 1.0 + sq * (-1.2337005501 + sq * (0.2536695079 + sq * (-0.0208634807 + sq * (0.00091926027 - sq * 0.0000252020424))))
    turns = whole.astype(jnp.int32)
    odd = (turns & 1) == 1
    sin_v = jnp.where(odd, cos_p, sin_p)
    cos_v = jnp.where(odd, sin_p, cos_p)
    sin_v = jnp.where((turns & 2) == 2, -sin_v, sin_v)
    cos_v = jnp.where(((turns + 1) & 2) == 2, -cos_v, cos_v)
    return sin_v, cos_v


def fused_kernel(
    devices, planes, own, segs,
    freq_ref, sig_ref, cot_ref, pick_ref, outer_any, inner_any, twist_any,
    wemb_ref, bias_ref, wout_ref, decay_ref,
    conv_ref, dsig_ref, gemb_ref, gbias_ref, gcol_ref,
    send_a, recv_a, send_b, recv_b, hid_ref, cos_ref, taps_ref, draw_ref,
    outer_ref, inner_ref, twist_ref, wmix_ref, rot_ref, tone_ref, wrow_ref, wcol_ref,
    gout_ref, gmix_ref, square_ref, send_c, recv_c, send_d, recv_d,
    send_sem, recv_sem, send_sem_d, recv_sem_d, load_sem,
):
    bf = jnp.bfloat16
    me = lax.axis_index("seq")
    blocks = devices * segs
    rows = blocks * own
    part = segs * own
    seq_total = blocks * WIDE
    per = WIDE // 64
    groups = blocks // per
    barrier = pltpu.get_barrier_semaphore()

    lane_id = lax.axis_index("chan")
    everyone = devices * planes
    mine = lane_id * devices + me

    def greet(step, carry):
        peer = lax.rem(mine + step, everyone)
        pl.semaphore_signal(
            barrier, inc=1,
            device_id={"seq": lax.rem(peer, devices), "chan": peer // devices},
            device_id_type=pl.DeviceIdType.MESH,
        )
        return carry

    lax.fori_loop(1, everyone, greet, 0)
    loads = [
        pltpu.make_async_copy(src, dst, load_sem.at[i])
        for i, (src, dst) in enumerate(
            [(outer_any, outer_ref), (inner_any, inner_ref), (twist_any, twist_ref)]
        )
    ]
    for load in loads:
        load.start()

    def copy_of(phase, src, dst, step):
        peer = lax.rem(me + step, devices)
        return pltpu.make_async_remote_copy(
            src_ref=src.at[peer],
            dst_ref=dst.at[me],
            send_sem=send_sem.at[phase, step],
            recv_sem=recv_sem.at[phase, step],
            device_id={"seq": peer},
            device_id_type=pl.DeviceIdType.MESH,
        )

    def start_all(phase, src, dst):
        def body(step, carry):
            copy_of(phase, src, dst, step).start()
            return carry

        lax.fori_loop(1, devices, body, 0)

    def wait_all(phase, src, dst):
        def body(step, carry):
            copy_of(phase, src, dst, step).wait()
            return carry

        lax.fori_loop(1, devices, body, 0)

    def pack(x_ref, at):
        wide = jnp.concatenate([x_ref[q * HALF:(q + 1) * HALF, :] for q in range(segs)], axis=1)
        mixed = jnp.concatenate([dot_nt(pick_ref[h], wide) for h in range(2)], axis=1)
        send_a[:, at:at + part, :] = mixed.astype(bf).reshape(devices, part, WIDE)

    pack(sig_ref, 0)
    pack(cot_ref, part)
    pl.semaphore_wait(barrier, everyone - 1)
    start_all(0, send_a, recv_a)
    recv_a[me] = send_a[me]

    turn_scale = 4.0 / seq_total
    far_lane = lax.broadcasted_iota(jnp.int32, (blocks, HALF), 1)
    far_row = lax.broadcasted_iota(jnp.int32, (blocks, HALF), 0)
    near_row = lax.broadcasted_iota(jnp.int32, (HALF, WIDE), 0)
    near_lane = lax.broadcasted_iota(jnp.int32, (HALF, WIDE), 1)
    lane_row = lax.broadcasted_iota(jnp.int32, (1, HALF), 1)
    lane_col = lax.broadcasted_iota(jnp.int32, (HALF, 1), 0)
    freq_row = jnp.zeros((1, HALF), jnp.int32)
    freq_col = jnp.zeros((HALF, 1), jnp.int32)
    for j in range(16):
        freq_row = jnp.where((lane_row & 15) == j, freq_ref[j], freq_row)
        freq_col = jnp.where((lane_col & 15) == j, freq_ref[j], freq_col)
    wrapped = (far_row * WIDE * freq_row) & (seq_total - 1)
    far_s, far_c = sin_cos(wrapped.astype(jnp.float32) * turn_scale)
    live = far_lane < 96
    rot_ref[0] = jnp.where(live, far_c, jnp.where(far_lane < 98, 1.0, 0.0))
    rot_ref[1] = jnp.where(live, jnp.where((far_lane & 16) == 0, far_s, -far_s), 0.0)
    spot = 2 * (near_lane & (HALF - 1)) + (near_lane >> 7)
    wrapped = (spot * freq_col) & (seq_total - 1)
    near_s, near_c = sin_cos(wrapped.astype(jnp.float32) * turn_scale)
    tone = jnp.where((near_row & 16) == 0, near_c, near_s)
    tone_hi = tone.astype(bf).astype(jnp.float32)
    tone = jnp.where((near_row >= 32) & (near_row < 64), tone - tone_hi, tone_hi)
    tone = jnp.where(near_row < 96, tone, jnp.where(near_row < 98, 1.0, 0.0))
    tone_ref[...] = tone.astype(bf)
    quarter_of = 2.0 / math.pi
    two_rows = lax.broadcasted_iota(jnp.int32, (8, 64), 0) < 2
    for side in range(2):
        square_ref[...] = jnp.zeros_like(square_ref)
        for rep in range(3):
            for half in range(2):
                at_row = rep * 32 + 16 * (half ^ side)
                square_ref[at_row:at_row + 16, 0:64] = wemb_ref[half * 16:half * 16 + 16, :] * quarter_of
        if side == 0:
            square_ref[96:104, 0:64] = jnp.where(two_rows, bias_ref[...] * quarter_of, 0.0)
        wmix_ref[side] = square_ref[...].T[0:64, :]
    per_own = per * own
    w_all = wout_ref[...]
    w_hi = w_all.astype(bf)
    w_lo = (w_all - w_hi.astype(jnp.float32)).astype(bf)
    chans = devices * own
    chan_at = lax.broadcasted_iota(jnp.int32, (per_own, chans), 1)
    chan_row = lax.broadcasted_iota(jnp.int32, (per_own, chans), 0)
    one_hot = jnp.where(chan_at == me * own + chan_row % own, 1.0, 0.0).astype(bf)
    row_keep = lax.broadcasted_iota(jnp.int32, (per_own, WIDE), 0) // own
    row_keep = row_keep == lax.broadcasted_iota(jnp.int32, (per_own, WIDE), 1) // 64
    col_keep = lax.broadcasted_iota(jnp.int32, (WIDE, per_own), 1) // own
    col_keep = col_keep == lax.broadcasted_iota(jnp.int32, (WIDE, per_own), 0) // 64
    for side, w_part in enumerate((w_hi, w_lo)):
        w_rep = jnp.concatenate([w_part] * per, axis=0)
        wrow_ref[side * per_own:(side + 1) * per_own, :] = jnp.where(
            row_keep, dot_nt(one_hot, w_rep), 0.0
        ).astype(bf)
        wcol_ref[side] = jnp.where(col_keep, dot_nt(w_rep, one_hot), 0.0).astype(bf)
    rate_at = lax.broadcasted_iota(jnp.int32, (rows, chans), 1)
    rate_row = lax.broadcasted_iota(jnp.int32, (rows, chans), 0)
    rate = jnp.sum(
        jnp.where(rate_at == me * own + rate_row % own, decay_ref[...], 0.0), axis=1, keepdims=True
    )
    peak = jnp.sqrt((1.0 + rate) / seq_total)

    lanes = lax.broadcasted_iota(jnp.int32, (64, HALF), 1)
    high_lane = (lanes < 64) | (lanes == 97)

    def net_step(g, carry):
        mixes = []
        for b in range(per):
            turn_c = rot_ref[0, pl.ds(g * per + b, 1), :]
            turn_s = rot_ref[1, pl.ds(g * per + b, 1), :]
            mix = wmix_ref[0] * turn_c + wmix_ref[1] * turn_s
            top = mix.astype(bf).astype(jnp.float32)
            mixes.append(jnp.where(high_lane, top, mix - top).astype(bf))
        quarter = dot_nn(jnp.concatenate(mixes, axis=0), tone_ref[...])
        sin_v, cos_v = sin_cos(quarter)
        hid = sin_v.astype(bf)
        at = pl.multiple_of(g * WIDE, WIDE)
        hid_ref[pl.ds(at, WIDE), :] = hid
        cos_ref[pl.ds(at, WIDE), :] = cos_v.astype(bf)
        both = dot_nn(wrow_ref[...], hid)
        taps_ref[pl.ds(pl.multiple_of(g * per * own, per * own), per * own), :] = (
            both[:per * own] + both[per * own:]
        )
        return carry

    lax.fori_loop(0, groups, net_step, 0)
    row_at = lax.broadcasted_iota(jnp.int32, (rows, WIDE), 0) // own
    lane_at = lax.broadcasted_iota(jnp.int32, (rows, WIDE), 1)
    fraction = (row_at * WIDE + 2 * (lane_at % HALF) + lane_at // HALF).astype(jnp.float32) / seq_total
    envelope = jnp.exp(-rate * fraction) * peak
    taps = taps_ref[...] * envelope

    for load in loads:
        load.wait()
    cos_t = twist_ref[0]
    sin_t = twist_ref[1]

    def rest_of(stage_r, stage_i):
        return jnp.concatenate(
            [stage_r * cos_t + stage_i * sin_t, stage_i * cos_t - stage_r * sin_t], axis=1
        ).astype(bf)

    def inner_fwd(turned):
        spec = dot_nn(turned, inner_ref[0]) + dot_nn(turned, inner_ref[1])
        return spec[:, :WIDE], spec[:, WIDE:]

    tap_hi = taps.astype(bf)
    tap_lo = (taps - tap_hi.astype(jnp.float32)).astype(bf)
    st = dot_nn(outer_ref[0], tap_hi) + dot_nn(outer_ref[1], tap_hi) + dot_nn(outer_ref[0], tap_lo)
    tap_r, tap_i = inner_fwd(rest_of(st[:rows], st[rows:]))

    wait_all(0, send_a, recv_a)

    def fwd(at):
        x = recv_a[:, at:at + part, :].reshape(rows, WIDE)
        stage = dot_nn(outer_ref[0], x) + dot_nn(outer_ref[1], x)
        return inner_fwd(rest_of(stage[:rows], stage[rows:]))

    sig_r, sig_i = fwd(0)
    cot_r, cot_i = fwd(part)

    def back(spec_r, spec_i):
        spec = jnp.concatenate([spec_r, spec_i], axis=1).astype(bf)
        time = dot_nt(spec, inner_ref[0]) + dot_nt(spec, inner_ref[1])
        time_r, time_i = time[:, :WIDE], time[:, WIDE:]
        turned = jnp.concatenate(
            [time_r * cos_t - time_i * sin_t, time_i * cos_t + time_r * sin_t], axis=0
        ).astype(bf)
        return (dot_tn(outer_ref[0], turned) + dot_tn(outer_ref[1], turned)) * (1.0 / seq_total)

    out = back(sig_r * tap_r - sig_i * tap_i, sig_r * tap_i + sig_i * tap_r)
    send_b[:, 0:part, :] = out.astype(bf).reshape(devices, part, WIDE)
    out = back(cot_r * tap_r + cot_i * tap_i, cot_i * tap_r - cot_r * tap_i)
    send_b[:, part:2 * part, :] = out.astype(bf).reshape(devices, part, WIDE)
    start_all(1, send_b, recv_b)
    recv_b[me] = send_b[me]

    d_taps = back(cot_r * sig_r + cot_i * sig_i, cot_i * sig_r - cot_r * sig_i)
    draw_ref[...] = (d_taps * envelope).astype(bf)
    gout_ref[...] = jnp.zeros_like(gout_ref)
    gmix_ref[...] = jnp.zeros_like(gmix_ref)

    def grad_step(g, carry):
        at = pl.multiple_of(g * WIDE, WIDE)
        d_raw = draw_ref[pl.ds(pl.multiple_of(g * per * own, per * own), per * own), :]
        gout_ref[...] += dot_nt(d_raw, hid_ref[pl.ds(at, WIDE), :])
        d_hid = dot_nn(wcol_ref[0], d_raw) + dot_nn(wcol_ref[1], d_raw)
        d_pre = (d_hid * cos_ref[pl.ds(at, WIDE), :].astype(jnp.float32)).astype(bf)
        d_mix = dot_nt(d_pre, tone_ref[...])
        for b in range(per):
            turn_c = rot_ref[0, pl.ds(g * per + b, 1), :]
            turn_s = rot_ref[1, pl.ds(g * per + b, 1), :]
            piece = d_mix[b * 64:(b + 1) * 64, :]
            gmix_ref[0] += piece * turn_c
            gmix_ref[1] += piece * turn_s
        return carry

    lax.fori_loop(0, groups, grad_step, 0)

    mix_lane = lax.broadcasted_iota(jnp.int32, (64, HALF), 1)
    mix_s = gmix_ref[1]
    crossed = jnp.where(
        mix_lane < 16, pltpu.roll(mix_s, HALF - 16, 1),
        jnp.where(mix_lane < 32, pltpu.roll(mix_s, 16, 1), 0.0),
    )
    square_ref[0:64, :] = gmix_ref[0] + crossed
    keep = jnp.where(row_keep, gout_ref[...], 0.0)
    keep = keep[:, :HALF] + keep[:, HALF:]
    keep = keep + pltpu.roll(keep, 64, 1)
    square_ref[64:64 + per_own, :] = keep
    g_own = square_ref[64:64 + own, :]
    for b in range(1, per):
        g_own = g_own + square_ref[64 + b * own:64 + (b + 1) * own, :]
    for r in range(devices):
        send_c[r, 0:own, :] = square_ref[r * own:(r + 1) * own, :]
        send_c[r, own:2 * own, :] = g_own
    start_all(2, send_c, recv_c)
    recv_c[me] = send_c[me]
    wait_all(2, send_c, recv_c)
    summed = recv_c[0]
    for r in range(1, devices):
        summed = summed + recv_c[r]
    send_d[...] = summed

    def spread_of(step):
        peer = lax.rem(mine + step, everyone)
        return pltpu.make_async_remote_copy(
            src_ref=send_d,
            dst_ref=recv_d.at[mine],
            send_sem=send_sem_d.at[step],
            recv_sem=recv_sem_d.at[step],
            device_id={"seq": lax.rem(peer, devices), "chan": peer // devices},
            device_id_type=pl.DeviceIdType.MESH,
        )

    def spread_start(step, carry):
        spread_of(step).start()
        return carry

    def spread_wait(step, carry):
        spread_of(step).wait()
        return carry

    lax.fori_loop(1, everyone, spread_start, 0)
    recv_d[mine] = send_d[...]
    wait_all(1, send_b, recv_b)

    def unpack(o_ref, at):
        x = recv_b[:, at:at + part, :].reshape(rows, WIDE)
        wide = dot_tn(x[:, :HALF], pick_ref[0]) + dot_tn(x[:, HALF:], pick_ref[1])
        for q in range(segs):
            o_ref[q * HALF:(q + 1) * HALF, :] = wide[:, q * HALF:(q + 1) * HALF].astype(bf)

    unpack(conv_ref, 0)
    unpack(dsig_ref, part)
    lax.fori_loop(1, everyone, spread_wait, 0)
    for r in range(devices):
        total = recv_d[r]
        for other in range(1, planes):
            total = total + recv_d[other * devices + r]
        square_ref[r * own:(r + 1) * own, :] = total[0:own, :]
        square_ref[64 + r * own:64 + (r + 1) * own, :] = recv_c[r, own:2 * own, :]
    flipped = square_ref[...].T * (1.0 / math.sqrt(seq_total))
    gemb_ref[...] = flipped[0:32, 0:64]
    gbias_ref[...] = flipped[96:97, 0:64]
    gcol_ref[...] = flipped[0:64, 64:128]


def local(signal, cotangent, band_freq, w_embed, b_embed, w_out, decay):
    devices = lax.axis_size("seq")
    me = lax.axis_index("seq")
    seg_len = signal.shape[1] * 2
    chans = signal.shape[2] // 2
    own = chans // devices
    if (
        chans % devices or seg_len % WIDE or own != 4 or seg_len * devices & (seg_len * devices - 1)
        or seg_len * devices * 2048 > 2**30
        or w_embed.shape != (32, 64) or chans * 2 != HALF
    ):
        return local_any(signal, cotangent, band_freq, w_embed, b_embed, w_out, decay)
    segs = seg_len // WIDE
    blocks = devices * segs
    rows = blocks * own
    seq_total = seg_len * devices
    bf, f32 = jnp.bfloat16, jnp.float32
    hidden = 64
    per = WIDE // hidden
    planes = lax.axis_size("chan")
    outer, inner, twist, pick = const_tables(devices, own, segs)
    part = segs * own
    vmem = pl.BlockSpec(memory_space=pltpu.VMEM)
    away = pl.BlockSpec(memory_space=pl.ANY)
    conv, dsig, g_emb, g_bias, g_out = pl.pallas_call(
        functools.partial(fused_kernel, devices, planes, own, segs),
        out_shape=(
            jax.ShapeDtypeStruct(signal.shape[1:], bf),
            jax.ShapeDtypeStruct(signal.shape[1:], bf),
            jax.ShapeDtypeStruct((32, hidden), f32),
            jax.ShapeDtypeStruct((1, hidden), f32),
            jax.ShapeDtypeStruct((hidden, chans), f32),
        ),
        in_specs=[pl.BlockSpec(memory_space=pltpu.SMEM)] + [vmem] * 3 + [away] * 3 + [vmem] * 4,
        out_specs=(vmem,) * 5,
        scratch_shapes=[pltpu.VMEM((devices, 2 * part, WIDE), bf)] * 4
        + [pltpu.VMEM((blocks * hidden, WIDE), bf)] * 2
        + [
            pltpu.VMEM((rows, WIDE), f32),
            pltpu.VMEM((rows, WIDE), bf),
            pltpu.VMEM(outer.shape, bf),
            pltpu.VMEM(inner.shape, bf),
            pltpu.VMEM(twist.shape, f32),
            pltpu.VMEM((2, hidden, HALF), f32),
            pltpu.VMEM((2, blocks, HALF), f32),
            pltpu.VMEM((HALF, WIDE), bf),
            pltpu.VMEM((2 * per * own, WIDE), bf),
            pltpu.VMEM((2, WIDE, per * own), bf),
            pltpu.VMEM((per * own, WIDE), f32),
            pltpu.VMEM((2, hidden, HALF), f32),
            pltpu.VMEM((HALF, HALF), f32),
            pltpu.VMEM((devices, 2 * own, HALF), f32),
            pltpu.VMEM((devices, 2 * own, HALF), f32),
            pltpu.VMEM((2 * own, HALF), f32),
            pltpu.VMEM((devices * planes, 2 * own, HALF), f32),
            pltpu.SemaphoreType.DMA((3, devices)),
            pltpu.SemaphoreType.DMA((3, devices)),
            pltpu.SemaphoreType.DMA((devices * planes,)),
            pltpu.SemaphoreType.DMA((devices * planes,)),
            pltpu.SemaphoreType.DMA((3,)),
        ],
        compiler_params=pltpu.CompilerParams(
            collective_id=0, has_side_effects=True, vmem_limit_bytes=56 * 2**20
        ),
    )(
        band_freq, signal[0], cotangent[0], jnp.asarray(pick), jnp.asarray(outer),
        jnp.asarray(inner), jnp.asarray(twist), w_embed, b_embed[None, :], w_out, decay[None, :],
    )
    return (conv[None], dsig[None], g_emb, g_bias[0], g_out)


def solution(mesh):
    return jax.shard_map(
        local,
        mesh=mesh,
        in_specs=(
            P("chan", "seq", None),
            P("chan", "seq", None),
            P(),
            P(),
            P(),
            P(None, "chan"),
            P("chan"),
        ),
        out_specs=(P("chan", "seq", None), P("chan", "seq", None), P(), P(), P(None, "chan")),
        check_vma=False,
    )
```

```python
import functools
import math

import jax
import jax.numpy as jnp
import numpy as np
from jax import lax
from jax.experimental import pallas as pl
from jax.experimental.pallas import tpu as pltpu
from jax.sharding import PartitionSpec as P

exact_mode = lax.Precision.HIGHEST


def mat_dot(lhs_mat, rhs_mat):
    return jnp.dot(lhs_mat, rhs_mat, preferred_element_type=jnp.float32, precision=exact_mode)


def side_dot(table, values):
    return jnp.einsum(
        "db,cbm->cdm", table, values, preferred_element_type=jnp.float32, precision=exact_mode
    )


def inner_dot(table, values):
    return jnp.einsum(
        "eb,cdbh->cdeh", table, values, preferred_element_type=jnp.float32, precision=exact_mode
    )


def band_phase(band_freq, places, seq_total):
    upper_part = places // 1024
    lower_part = places % 1024
    partial_turn = upper_part[:, None] * band_freq[None, :] % seq_total
    wrapped = (partial_turn * 1024 + lower_part[:, None] * band_freq[None, :]) % seq_total
    return wrapped.astype(jnp.float32) * (2.0 * math.pi / seq_total)


def filter_parts(places, band_freq, w_embed, b_embed, w_out, decay, seq_total):
    phases = band_phase(band_freq, places, seq_total)
    features = jnp.concatenate([jnp.cos(phases), jnp.sin(phases)], axis=1)
    preact = mat_dot(features, w_embed) + b_embed[None, :]
    hidden = jnp.sin(preact)
    fraction = places.astype(jnp.float32) / seq_total
    envelope = (
        jnp.exp(-decay[None, :] * fraction[:, None]) * jnp.sqrt((1.0 + decay) / seq_total)[None, :]
    )
    taps = mat_dot(hidden, w_out) * envelope
    return (features, preact, hidden, taps, envelope)


def angle_table(rows_idx, cols_idx, modulus):
    wrapped = rows_idx[:, None] * cols_idx[None, :] % modulus
    angles = wrapped.astype(jnp.float32) * (2.0 * math.pi / modulus)
    return (jnp.cos(angles), jnp.sin(angles))


def local_any(signal, cotangent, band_freq, w_embed, b_embed, w_out, decay):
    devices = lax.axis_size("seq")
    rank_seq = lax.axis_index("seq")
    seg_len = signal.shape[1] * 2
    channels = signal.shape[2] // 2
    block_w = seg_len // devices
    rows_all = 2 * devices
    seq_total = seg_len * devices
    fft_size = 2 * seq_total
    inv_scale = 1.0 / fft_size
    radix_one = max(
        (divisor for divisor in range(1, math.isqrt(seg_len) + 1) if seg_len % divisor == 0)
    )
    radix_two = seg_len // radix_one
    row_ids = jnp.arange(rows_all, dtype=jnp.int32)
    src_ids = jnp.arange(devices, dtype=jnp.int32)
    col_glob = rank_seq * block_w + jnp.arange(block_w, dtype=jnp.int32)
    seg_ids = jnp.arange(seg_len, dtype=jnp.int32)
    one_ids = jnp.arange(radix_one, dtype=jnp.int32)
    two_ids = jnp.arange(radix_two, dtype=jnp.int32)
    pair_ids = lax.dynamic_slice_in_dim(row_ids, 2 * rank_seq, 2)
    outer_cos, outer_sin = angle_table(row_ids, src_ids, rows_all)
    entry_cos, entry_sin = angle_table(row_ids, col_glob, fft_size)
    first_cos, first_sin = angle_table(one_ids, one_ids, radix_one)
    second_cos, second_sin = angle_table(two_ids, two_ids, radix_two)
    inner_cos, inner_sin = angle_table(one_ids, two_ids, seg_len)
    exit_cos, exit_sin = angle_table(pair_ids, seg_ids, fft_size)
    inner_c = inner_cos[None, :, :, None]
    inner_s = inner_sin[None, :, :, None]

    def twist_stack(real_a, imag_a):
        real_a = real_a.reshape(rows_all, block_w, channels)
        imag_a = imag_a.reshape(rows_all, block_w, channels)
        twist_c = entry_cos[:, :, None]
        twist_s = entry_sin[:, :, None]
        real_b = real_a * twist_c + imag_a * twist_s
        imag_b = imag_a * twist_c - real_a * twist_s
        return jnp.stack([real_b, imag_b]).reshape(2, rows_all, block_w * channels)

    def column_pass(cols_data):
        return twist_stack(mat_dot(outer_cos, cols_data), -mat_dot(outer_sin, cols_data))

    def local_forward(stacked):
        grid = stacked.reshape(2, 2, radix_one, radix_two * channels)
        part_r = side_dot(first_cos, grid[0]) + side_dot(first_sin, grid[1])
        part_i = side_dot(first_cos, grid[1]) - side_dot(first_sin, grid[0])
        part_r = part_r.reshape(2, radix_one, radix_two, channels)
        part_i = part_i.reshape(2, radix_one, radix_two, channels)
        turn_r = part_r * inner_c + part_i * inner_s
        turn_i = part_i * inner_c - part_r * inner_s
        spec_r = inner_dot(second_cos, turn_r) + inner_dot(second_sin, turn_i)
        spec_i = inner_dot(second_cos, turn_i) - inner_dot(second_sin, turn_r)
        return (spec_r, spec_i)

    def local_inverse(spec_r, spec_i):
        back_r = inner_dot(second_cos, spec_r) - inner_dot(second_sin, spec_i)
        back_i = inner_dot(second_cos, spec_i) + inner_dot(second_sin, spec_r)
        turn_r = (back_r * inner_c - back_i * inner_s).reshape(2, radix_one, radix_two * channels)
        turn_i = (back_r * inner_s + back_i * inner_c).reshape(2, radix_one, radix_two * channels)
        time_r = (side_dot(first_cos, turn_r) - side_dot(first_sin, turn_i)).reshape(
            2, seg_len, channels
        )
        time_i = (side_dot(first_cos, turn_i) + side_dot(first_sin, turn_r)).reshape(
            2, seg_len, channels
        )
        twist_c = exit_cos[:, :, None]
        twist_s = exit_sin[:, :, None]
        final_r = time_r * twist_c - time_i * twist_s
        final_i = time_r * twist_s + time_i * twist_c
        return jnp.stack([final_r, final_i]).reshape(2, 2, seg_len * channels)

    def real_rows(gathered):
        return mat_dot(outer_cos.T, gathered[0]) - mat_dot(outer_sin.T, gathered[1])

    sig_cols, cot_cols = (
        lax.all_to_all(
            signal.reshape(devices, block_w * channels),
            "seq",
            split_axis=0,
            concat_axis=0,
            tiled=True,
        ),
        lax.all_to_all(
            cotangent.reshape(devices, block_w * channels),
            "seq",
            split_axis=0,
            concat_axis=0,
            tiled=True,
        ),
    )
    places = rank_seq * seg_len + seg_ids
    features, preact, hidden, taps, envelope = filter_parts(
        places, band_freq, w_embed, b_embed, w_out, decay, seq_total
    )
    tap_cols = lax.all_to_all(
        taps.reshape(devices, block_w * channels), "seq", split_axis=0, concat_axis=0, tiled=True
    )
    spec_sig, spec_cot, spec_tap = (
        lax.all_to_all(
            column_pass(sig_cols.astype(jnp.float32)),
            "seq",
            split_axis=1,
            concat_axis=2,
            tiled=True,
        ),
        lax.all_to_all(
            column_pass(cot_cols.astype(jnp.float32)),
            "seq",
            split_axis=1,
            concat_axis=2,
            tiled=True,
        ),
        lax.all_to_all(column_pass(tap_cols), "seq", split_axis=1, concat_axis=2, tiled=True),
    )
    sig_r, sig_i = local_forward(spec_sig)
    cot_r, cot_i = local_forward(spec_cot)
    tap_r, tap_i = local_forward(spec_tap)
    prod_r = sig_r * tap_r - sig_i * tap_i
    prod_i = sig_r * tap_i + sig_i * tap_r
    grad_r = cot_r * tap_r + cot_i * tap_i
    grad_i = cot_i * tap_r - cot_r * tap_i
    corr_r = cot_r * sig_r + cot_i * sig_i
    corr_i = cot_i * sig_r - cot_r * sig_i
    prod_back, grad_back, corr_back = (
        lax.all_to_all(
            local_inverse(prod_r, prod_i), "seq", split_axis=2, concat_axis=1, tiled=True
        ),
        lax.all_to_all(
            local_inverse(grad_r, grad_i), "seq", split_axis=2, concat_axis=1, tiled=True
        ),
        lax.all_to_all(
            local_inverse(corr_r, corr_i), "seq", split_axis=2, concat_axis=1, tiled=True
        ),
    )
    out_cols = real_rows(prod_back)
    dsig_cols = real_rows(grad_back)
    dtap_cols = real_rows(corr_back) * inv_scale
    out_rows, dsig_rows = (
        lax.all_to_all(
            (out_cols * inv_scale).astype(jnp.bfloat16),
            "seq",
            split_axis=0,
            concat_axis=0,
            tiled=True,
        ),
        lax.all_to_all(
            (dsig_cols * inv_scale).astype(jnp.bfloat16),
            "seq",
            split_axis=0,
            concat_axis=0,
            tiled=True,
        ),
    )
    conv_out = out_rows.reshape(1, seg_len // 2, 2 * channels)
    d_signal = dsig_rows.reshape(1, seg_len // 2, 2 * channels)
    d_taps = (
        lax.all_to_all(
            dtap_cols.astype(jnp.bfloat16), "seq", split_axis=0, concat_axis=0, tiled=True
        )
        .astype(dtap_cols.dtype)
        .reshape(seg_len, channels)
    )
    d_raw = d_taps * envelope
    d_preact = mat_dot(d_raw, w_out.T) * jnp.cos(preact)
    out_part = mat_dot(hidden.T, d_raw)
    embed_part = mat_dot(features.T, d_preact)
    bias_part = jnp.sum(d_preact, axis=0)
    out_sum, embed_sum, bias_sum = lax.psum((out_part, embed_part, bias_part), "seq")
    embed_all, bias_all = lax.psum((embed_sum, bias_sum), "chan")
    norm_scale = 1.0 / math.sqrt(seq_total)
    return (conv_out, d_signal, embed_all * norm_scale, bias_all * norm_scale, out_sum * norm_scale)


WIDE = 256
HALF = 128


def split_np(table):
    high = table.astype(jnp.bfloat16)
    low = (table - high.astype(np.float64)).astype(jnp.bfloat16)
    return np.stack([high, low])


def const_tables(devices, own, segs):
    blocks = devices * segs
    total = 2 * blocks * WIDE
    eye = np.eye(own)
    half_f = np.arange(blocks) + 0.5
    alpha = 2 * np.pi * half_f[:, None] * np.arange(blocks)[None, :] / (2 * blocks)
    outer = np.concatenate([np.kron(np.cos(alpha), eye), np.kron(-np.sin(alpha), eye)])
    lane = np.arange(WIDE)
    places = 2 * (lane % HALF) + lane // HALF
    theta = np.repeat(2 * np.pi * half_f[:, None] * places[None, :] / total, own, axis=0)
    twist = np.stack([np.cos(theta), np.sin(theta)]).astype(np.float32)
    phi = 2 * np.pi * (places[:, None] * np.arange(WIDE)[None, :] % WIDE) / WIDE
    inner = np.block([[np.cos(phi), -np.sin(phi)], [np.sin(phi), np.cos(phi)]])
    chans = devices * own
    pick = np.zeros((2, devices, segs, own, segs, 2, chans), np.float32)
    for h in range(2):
        for r in range(devices):
            for q in range(segs):
                for k in range(own):
                    pick[h, r, q, k, q, h, r * own + k] = 1.0
    pick = pick.reshape(2, devices * segs * own, segs * 2 * chans).astype(jnp.bfloat16)
    return split_np(outer), split_np(inner), twist, pick


def dot_nn(lhs, rhs):
    return lax.dot_general(lhs, rhs, (((1,), (0,)), ((), ())), preferred_element_type=jnp.float32)


def dot_nt(lhs, rhs):
    return lax.dot_general(lhs, rhs, (((1,), (1,)), ((), ())), preferred_element_type=jnp.float32)


def dot_tn(lhs, rhs):
    return lax.dot_general(lhs, rhs, (((0,), (0,)), ((), ())), preferred_element_type=jnp.float32)


def sin_cos(quarter):
    whole = jnp.round(quarter)
    rest = quarter - whole
    sq = rest * rest
    sin_p = rest * (1.5707963268 + sq * (-0.6459640975 + sq * (0.0796926262 + sq * (-0.0046817541 + sq * 0.00016044118))))
    cos_p = 1.0 + sq * (-1.2337005501 + sq * (0.2536695079 + sq * (-0.0208634807 + sq * (0.00091926027 - sq * 0.0000252020424))))
    turns = whole.astype(jnp.int32)
    odd = (turns & 1) == 1
    sin_v = jnp.where(odd, cos_p, sin_p)
    cos_v = jnp.where(odd, sin_p, cos_p)
    sin_v = jnp.where((turns & 2) == 2, -sin_v, sin_v)
    cos_v = jnp.where(((turns + 1) & 2) == 2, -cos_v, cos_v)
    return sin_v, cos_v


def fused_kernel(
    devices, planes, own, segs,
    freq_ref, sig_ref, cot_ref, pick_ref, outer_any, inner_any, twist_any,
    wemb_ref, bias_ref, wout_ref, decay_ref,
    conv_ref, dsig_ref, gemb_ref, gbias_ref, gcol_ref,
    send_a, recv_a, send_b, recv_b, hid_ref, cos_ref, taps_ref, draw_ref,
    outer_ref, inner_ref, twist_ref, wmix_ref, rot_ref, tone_ref, wrow_ref, wcol_ref,
    gout_ref, gmix_ref, square_ref, send_c, recv_c, send_d, recv_d,
    send_sem, recv_sem, send_sem_d, recv_sem_d, load_sem,
):
    bf = jnp.bfloat16
    me = lax.axis_index("seq")
    blocks = devices * segs
    rows = blocks * own
    part = segs * own
    seq_total = blocks * WIDE
    per = WIDE // 64
    groups = blocks // per
    barrier = pltpu.get_barrier_semaphore()

    lane_id = lax.axis_index("chan")
    everyone = devices * planes
    mine = lane_id * devices + me

    def greet(step, carry):
        peer = lax.rem(mine + step, everyone)
        pl.semaphore_signal(
            barrier, inc=1,
            device_id={"seq": lax.rem(peer, devices), "chan": peer // devices},
            device_id_type=pl.DeviceIdType.MESH,
        )
        return carry

    lax.fori_loop(1, everyone, greet, 0)
    loads = [
        pltpu.make_async_copy(src, dst, load_sem.at[i])
        for i, (src, dst) in enumerate(
            [(outer_any, outer_ref), (inner_any, inner_ref), (twist_any, twist_ref)]
        )
    ]
    for load in loads:
        load.start()

    def copy_of(phase, src, dst, step):
        peer = lax.rem(me + step, devices)
        return pltpu.make_async_remote_copy(
            src_ref=src.at[peer],
            dst_ref=dst.at[me],
            send_sem=send_sem.at[phase, step],
            recv_sem=recv_sem.at[phase, step],
            device_id={"seq": peer},
            device_id_type=pl.DeviceIdType.MESH,
        )

    def start_all(phase, src, dst):
        def body(step, carry):
            copy_of(phase, src, dst, step).start()
            return carry

        lax.fori_loop(1, devices, body, 0)

    def wait_all(phase, src, dst):
        def body(step, carry):
            copy_of(phase, src, dst, step).wait()
            return carry

        lax.fori_loop(1, devices, body, 0)

    def pack(x_ref, at):
        wide = jnp.concatenate([x_ref[q * HALF:(q + 1) * HALF, :] for q in range(segs)], axis=1)
        mixed = jnp.concatenate([dot_nt(pick_ref[h], wide) for h in range(2)], axis=1)
        send_a[:, at:at + part, :] = mixed.astype(bf).reshape(devices, part, WIDE)

    pack(sig_ref, 0)
    pack(cot_ref, part)
    pl.semaphore_wait(barrier, everyone - 1)
    start_all(0, send_a, recv_a)
    recv_a[me] = send_a[me]

    turn_scale = 4.0 / seq_total
    far_lane = lax.broadcasted_iota(jnp.int32, (blocks, HALF), 1)
    far_row = lax.broadcasted_iota(jnp.int32, (blocks, HALF), 0)
    near_row = lax.broadcasted_iota(jnp.int32, (HALF, WIDE), 0)
    near_lane = lax.broadcasted_iota(jnp.int32, (HALF, WIDE), 1)
    lane_row = lax.broadcasted_iota(jnp.int32, (1, HALF), 1)
    lane_col = lax.broadcasted_iota(jnp.int32, (HALF, 1), 0)
    freq_row = jnp.zeros((1, HALF), jnp.int32)
    freq_col = jnp.zeros((HALF, 1), jnp.int32)
    for j in range(16):
        freq_row = jnp.where((lane_row & 15) == j, freq_ref[j], freq_row)
        freq_col = jnp.where((lane_col & 15) == j, freq_ref[j], freq_col)
    wrapped = (far_row * WIDE * freq_row) & (seq_total - 1)
    far_s, far_c = sin_cos(wrapped.astype(jnp.float32) * turn_scale)
    live = far_lane < 96
    rot_ref[0] = jnp.where(live, far_c, jnp.where(far_lane < 98, 1.0, 0.0))
    rot_ref[1] = jnp.where(live, jnp.where((far_lane & 16) == 0, far_s, -far_s), 0.0)
    spot = 2 * (near_lane & (HALF - 1)) + (near_lane >> 7)
    wrapped = (spot * freq_col) & (seq_total - 1)
    near_s, near_c = sin_cos(wrapped.astype(jnp.float32) * turn_scale)
    tone = jnp.where((near_row & 16) == 0, near_c, near_s)
    tone_hi = tone.astype(bf).astype(jnp.float32)
    tone = jnp.where((near_row >= 32) & (near_row < 64), tone - tone_hi, tone_hi)
    tone = jnp.where(near_row < 96, tone, jnp.where(near_row < 98, 1.0, 0.0))
    tone_ref[...] = tone.astype(bf)
    quarter_of = 2.0 / math.pi
    two_rows = lax.broadcasted_iota(jnp.int32, (8, 64), 0) < 2
    for side in range(2):
        square_ref[...] = jnp.zeros_like(square_ref)
        for rep in range(3):
            for half in range(2):
                at_row = rep * 32 + 16 * (half ^ side)
                square_ref[at_row:at_row + 16, 0:64] = wemb_ref[half * 16:half * 16 + 16, :] * quarter_of
        if side == 0:
            square_ref[96:104, 0:64] = jnp.where(two_rows, bias_ref[...] * quarter_of, 0.0)
        wmix_ref[side] = square_ref[...].T[0:64, :]
    per_own = per * own
    w_all = wout_ref[...]
    w_hi = w_all.astype(bf)
    w_lo = (w_all - w_hi.astype(jnp.float32)).astype(bf)
    chans = devices * own
    chan_at = lax.broadcasted_iota(jnp.int32, (per_own, chans), 1)
    chan_row = lax.broadcasted_iota(jnp.int32, (per_own, chans), 0)
    one_hot = jnp.where(chan_at == me * own + chan_row % own, 1.0, 0.0).astype(bf)
    row_keep = lax.broadcasted_iota(jnp.int32, (per_own, WIDE), 0) // own
    row_keep = row_keep == lax.broadcasted_iota(jnp.int32, (per_own, WIDE), 1) // 64
    col_keep = lax.broadcasted_iota(jnp.int32, (WIDE, per_own), 1) // own
    col_keep = col_keep == lax.broadcasted_iota(jnp.int32, (WIDE, per_own), 0) // 64
    for side, w_part in enumerate((w_hi, w_lo)):
        w_rep = jnp.concatenate([w_part] * per, axis=0)
        wrow_ref[side * per_own:(side + 1) * per_own, :] = jnp.where(
            row_keep, dot_nt(one_hot, w_rep), 0.0
        ).astype(bf)
        wcol_ref[side] = jnp.where(col_keep, dot_nt(w_rep, one_hot), 0.0).astype(bf)
    rate_at = lax.broadcasted_iota(jnp.int32, (rows, chans), 1)
    rate_row = lax.broadcasted_iota(jnp.int32, (rows, chans), 0)
    rate = jnp.sum(
        jnp.where(rate_at == me * own + rate_row % own, decay_ref[...], 0.0), axis=1, keepdims=True
    )
    peak = jnp.sqrt((1.0 + rate) / seq_total)

    lanes = lax.broadcasted_iota(jnp.int32, (64, HALF), 1)
    high_lane = (lanes < 64) | (lanes == 97)

    def net_step(g, carry):
        mixes = []
        for b in range(per):
            turn_c = rot_ref[0, pl.ds(g * per + b, 1), :]
            turn_s = rot_ref[1, pl.ds(g * per + b, 1), :]
            mix = wmix_ref[0] * turn_c + wmix_ref[1] * turn_s
            top = mix.astype(bf).astype(jnp.float32)
            mixes.append(jnp.where(high_lane, top, mix - top).astype(bf))
        quarter = dot_nn(jnp.concatenate(mixes, axis=0), tone_ref[...])
        sin_v, cos_v = sin_cos(quarter)
        hid = sin_v.astype(bf)
        at = pl.multiple_of(g * WIDE, WIDE)
        hid_ref[pl.ds(at, WIDE), :] = hid
        cos_ref[pl.ds(at, WIDE), :] = cos_v.astype(bf)
        both = dot_nn(wrow_ref[...], hid)
        taps_ref[pl.ds(pl.multiple_of(g * per * own, per * own), per * own), :] = (
            both[:per * own] + both[per * own:]
        )
        return carry

    lax.fori_loop(0, groups, net_step, 0, unroll=4)
    row_at = lax.broadcasted_iota(jnp.int32, (rows, WIDE), 0) // own
    lane_at = lax.broadcasted_iota(jnp.int32, (rows, WIDE), 1)
    fraction = (row_at * WIDE + 2 * (lane_at % HALF) + lane_at // HALF).astype(jnp.float32) / seq_total
    envelope = jnp.exp(-rate * fraction) * peak
    taps = taps_ref[...] * envelope

    for load in loads:
        load.wait()
    cos_t = twist_ref[0]
    sin_t = twist_ref[1]

    def rest_of(stage_r, stage_i):
        return jnp.concatenate(
            [stage_r * cos_t + stage_i * sin_t, stage_i * cos_t - stage_r * sin_t], axis=1
        ).astype(bf)

    def inner_fwd(turned):
        spec = dot_nn(turned, inner_ref[0]) + dot_nn(turned, inner_ref[1])
        return spec[:, :WIDE], spec[:, WIDE:]

    tap_hi = taps.astype(bf)
    tap_lo = (taps - tap_hi.astype(jnp.float32)).astype(bf)
    st = dot_nn(outer_ref[0], tap_hi) + dot_nn(outer_ref[1], tap_hi) + dot_nn(outer_ref[0], tap_lo)
    tap_r, tap_i = inner_fwd(rest_of(st[:rows], st[rows:]))

    wait_all(0, send_a, recv_a)

    def fwd(at):
        x = recv_a[:, at:at + part, :].reshape(rows, WIDE)
        stage = dot_nn(outer_ref[0], x) + dot_nn(outer_ref[1], x)
        return inner_fwd(rest_of(stage[:rows], stage[rows:]))

    sig_r, sig_i = fwd(0)
    cot_r, cot_i = fwd(part)

    def back(spec_r, spec_i):
        spec = jnp.concatenate([spec_r, spec_i], axis=1).astype(bf)
        time = dot_nt(spec, inner_ref[0]) + dot_nt(spec, inner_ref[1])
        time_r, time_i = time[:, :WIDE], time[:, WIDE:]
        turned = jnp.concatenate(
            [time_r * cos_t - time_i * sin_t, time_i * cos_t + time_r * sin_t], axis=0
        ).astype(bf)
        return (dot_tn(outer_ref[0], turned) + dot_tn(outer_ref[1], turned)) * (1.0 / seq_total)

    out = back(sig_r * tap_r - sig_i * tap_i, sig_r * tap_i + sig_i * tap_r)
    send_b[:, 0:part, :] = out.astype(bf).reshape(devices, part, WIDE)
    out = back(cot_r * tap_r + cot_i * tap_i, cot_i * tap_r - cot_r * tap_i)
    send_b[:, part:2 * part, :] = out.astype(bf).reshape(devices, part, WIDE)
    start_all(1, send_b, recv_b)
    recv_b[me] = send_b[me]

    d_taps = back(cot_r * sig_r + cot_i * sig_i, cot_i * sig_r - cot_r * sig_i)
    draw_ref[...] = (d_taps * envelope).astype(bf)
    gout_ref[...] = jnp.zeros_like(gout_ref)
    gmix_ref[...] = jnp.zeros_like(gmix_ref)

    def grad_step(g, carry):
        at = pl.multiple_of(g * WIDE, WIDE)
        d_raw = draw_ref[pl.ds(pl.multiple_of(g * per * own, per * own), per * own), :]
        gout_ref[...] += dot_nt(d_raw, hid_ref[pl.ds(at, WIDE), :])
        d_hid = dot_nn(wcol_ref[0], d_raw) + dot_nn(wcol_ref[1], d_raw)
        d_pre = (d_hid * cos_ref[pl.ds(at, WIDE), :].astype(jnp.float32)).astype(bf)
        d_mix = dot_nt(d_pre, tone_ref[...])
        for b in range(per):
            turn_c = rot_ref[0, pl.ds(g * per + b, 1), :]
            turn_s = rot_ref[1, pl.ds(g * per + b, 1), :]
            piece = d_mix[b * 64:(b + 1) * 64, :]
            gmix_ref[0] += piece * turn_c
            gmix_ref[1] += piece * turn_s
        return carry

    lax.fori_loop(0, groups, grad_step, 0, unroll=4)

    mix_lane = lax.broadcasted_iota(jnp.int32, (64, HALF), 1)
    mix_s = gmix_ref[1]
    crossed = jnp.where(
        mix_lane < 16, pltpu.roll(mix_s, HALF - 16, 1),
        jnp.where(mix_lane < 32, pltpu.roll(mix_s, 16, 1), 0.0),
    )
    square_ref[0:64, :] = gmix_ref[0] + crossed
    keep = jnp.where(row_keep, gout_ref[...], 0.0)
    keep = keep[:, :HALF] + keep[:, HALF:]
    keep = keep + pltpu.roll(keep, 64, 1)
    square_ref[64:64 + per_own, :] = keep
    g_own = square_ref[64:64 + own, :]
    for b in range(1, per):
        g_own = g_own + square_ref[64 + b * own:64 + (b + 1) * own, :]
    for r in range(devices):
        send_c[r, 0:own, :] = square_ref[r * own:(r + 1) * own, :]
        send_c[r, own:2 * own, :] = g_own
    start_all(2, send_c, recv_c)
    recv_c[me] = send_c[me]
    wait_all(2, send_c, recv_c)
    summed = recv_c[0]
    for r in range(1, devices):
        summed = summed + recv_c[r]
    send_d[...] = summed

    def spread_of(step):
        peer = lax.rem(mine + step, everyone)
        return pltpu.make_async_remote_copy(
            src_ref=send_d,
            dst_ref=recv_d.at[mine],
            send_sem=send_sem_d.at[step],
            recv_sem=recv_sem_d.at[step],
            device_id={"seq": lax.rem(peer, devices), "chan": peer // devices},
            device_id_type=pl.DeviceIdType.MESH,
        )

    def spread_start(step, carry):
        spread_of(step).start()
        return carry

    def spread_wait(step, carry):
        spread_of(step).wait()
        return carry

    lax.fori_loop(1, everyone, spread_start, 0)
    recv_d[mine] = send_d[...]
    wait_all(1, send_b, recv_b)

    def unpack(o_ref, at):
        x = recv_b[:, at:at + part, :].reshape(rows, WIDE)
        wide = dot_tn(x[:, :HALF], pick_ref[0]) + dot_tn(x[:, HALF:], pick_ref[1])
        for q in range(segs):
            o_ref[q * HALF:(q + 1) * HALF, :] = wide[:, q * HALF:(q + 1) * HALF].astype(bf)

    unpack(conv_ref, 0)
    unpack(dsig_ref, part)
    lax.fori_loop(1, everyone, spread_wait, 0)
    for r in range(devices):
        total = recv_d[r]
        for other in range(1, planes):
            total = total + recv_d[other * devices + r]
        square_ref[r * own:(r + 1) * own, :] = total[0:own, :]
        square_ref[64 + r * own:64 + (r + 1) * own, :] = recv_c[r, own:2 * own, :]
    flipped = square_ref[...].T * (1.0 / math.sqrt(seq_total))
    gemb_ref[...] = flipped[0:32, 0:64]
    gbias_ref[...] = flipped[96:97, 0:64]
    gcol_ref[...] = flipped[0:64, 64:128]


def local(signal, cotangent, band_freq, w_embed, b_embed, w_out, decay):
    devices = lax.axis_size("seq")
    me = lax.axis_index("seq")
    seg_len = signal.shape[1] * 2
    chans = signal.shape[2] // 2
    own = chans // devices
    if (
        chans % devices or seg_len % WIDE or own != 4 or seg_len * devices & (seg_len * devices - 1)
        or seg_len * devices * 2048 > 2**30
        or w_embed.shape != (32, 64) or chans * 2 != HALF
    ):
        return local_any(signal, cotangent, band_freq, w_embed, b_embed, w_out, decay)
    segs = seg_len // WIDE
    blocks = devices * segs
    rows = blocks * own
    seq_total = seg_len * devices
    bf, f32 = jnp.bfloat16, jnp.float32
    hidden = 64
    per = WIDE // hidden
    planes = lax.axis_size("chan")
    outer, inner, twist, pick = const_tables(devices, own, segs)
    part = segs * own
    vmem = pl.BlockSpec(memory_space=pltpu.VMEM)
    away = pl.BlockSpec(memory_space=pl.ANY)
    conv, dsig, g_emb, g_bias, g_out = pl.pallas_call(
        functools.partial(fused_kernel, devices, planes, own, segs),
        out_shape=(
            jax.ShapeDtypeStruct(signal.shape[1:], bf),
            jax.ShapeDtypeStruct(signal.shape[1:], bf),
            jax.ShapeDtypeStruct((32, hidden), f32),
            jax.ShapeDtypeStruct((1, hidden), f32),
            jax.ShapeDtypeStruct((hidden, chans), f32),
        ),
        in_specs=[pl.BlockSpec(memory_space=pltpu.SMEM)] + [vmem] * 3 + [away] * 3 + [vmem] * 4,
        out_specs=(vmem,) * 5,
        scratch_shapes=[pltpu.VMEM((devices, 2 * part, WIDE), bf)] * 4
        + [pltpu.VMEM((blocks * hidden, WIDE), bf)] * 2
        + [
            pltpu.VMEM((rows, WIDE), f32),
            pltpu.VMEM((rows, WIDE), bf),
            pltpu.VMEM(outer.shape, bf),
            pltpu.VMEM(inner.shape, bf),
            pltpu.VMEM(twist.shape, f32),
            pltpu.VMEM((2, hidden, HALF), f32),
            pltpu.VMEM((2, blocks, HALF), f32),
            pltpu.VMEM((HALF, WIDE), bf),
            pltpu.VMEM((2 * per * own, WIDE), bf),
            pltpu.VMEM((2, WIDE, per * own), bf),
            pltpu.VMEM((per * own, WIDE), f32),
            pltpu.VMEM((2, hidden, HALF), f32),
            pltpu.VMEM((HALF, HALF), f32),
            pltpu.VMEM((devices, 2 * own, HALF), f32),
            pltpu.VMEM((devices, 2 * own, HALF), f32),
            pltpu.VMEM((2 * own, HALF), f32),
            pltpu.VMEM((devices * planes, 2 * own, HALF), f32),
            pltpu.SemaphoreType.DMA((3, devices)),
            pltpu.SemaphoreType.DMA((3, devices)),
            pltpu.SemaphoreType.DMA((devices * planes,)),
            pltpu.SemaphoreType.DMA((devices * planes,)),
            pltpu.SemaphoreType.DMA((3,)),
        ],
        compiler_params=pltpu.CompilerParams(
            collective_id=0, has_side_effects=True, vmem_limit_bytes=56 * 2**20
        ),
    )(
        band_freq, signal[0], cotangent[0], jnp.asarray(pick), jnp.asarray(outer),
        jnp.asarray(inner), jnp.asarray(twist), w_embed, b_embed[None, :], w_out, decay[None, :],
    )
    return (conv[None], dsig[None], g_emb, g_bias[0], g_out)


def solution(mesh):
    return jax.shard_map(
        local,
        mesh=mesh,
        in_specs=(
            P("chan", "seq", None),
            P("chan", "seq", None),
            P(),
            P(),
            P(),
            P(None, "chan"),
            P("chan"),
        ),
        out_specs=(P("chan", "seq", None), P("chan", "seq", None), P(), P(), P(None, "chan")),
        check_vma=False,
    )
```

```python
import functools
import math

import jax
import jax.numpy as jnp
import numpy as np
from jax import lax
from jax.experimental import pallas as pl
from jax.experimental.pallas import tpu as pltpu
from jax.sharding import PartitionSpec as P

exact_mode = lax.Precision.HIGHEST


def mat_dot(lhs_mat, rhs_mat):
    return jnp.dot(lhs_mat, rhs_mat, preferred_element_type=jnp.float32, precision=exact_mode)


def side_dot(table, values):
    return jnp.einsum(
        "db,cbm->cdm", table, values, preferred_element_type=jnp.float32, precision=exact_mode
    )


def inner_dot(table, values):
    return jnp.einsum(
        "eb,cdbh->cdeh", table, values, preferred_element_type=jnp.float32, precision=exact_mode
    )


def band_phase(band_freq, places, seq_total):
    upper_part = places // 1024
    lower_part = places % 1024
    partial_turn = upper_part[:, None] * band_freq[None, :] % seq_total
    wrapped = (partial_turn * 1024 + lower_part[:, None] * band_freq[None, :]) % seq_total
    return wrapped.astype(jnp.float32) * (2.0 * math.pi / seq_total)


def filter_parts(places, band_freq, w_embed, b_embed, w_out, decay, seq_total):
    phases = band_phase(band_freq, places, seq_total)
    features = jnp.concatenate([jnp.cos(phases), jnp.sin(phases)], axis=1)
    preact = mat_dot(features, w_embed) + b_embed[None, :]
    hidden = jnp.sin(preact)
    fraction = places.astype(jnp.float32) / seq_total
    envelope = (
        jnp.exp(-decay[None, :] * fraction[:, None]) * jnp.sqrt((1.0 + decay) / seq_total)[None, :]
    )
    taps = mat_dot(hidden, w_out) * envelope
    return (features, preact, hidden, taps, envelope)


def angle_table(rows_idx, cols_idx, modulus):
    wrapped = rows_idx[:, None] * cols_idx[None, :] % modulus
    angles = wrapped.astype(jnp.float32) * (2.0 * math.pi / modulus)
    return (jnp.cos(angles), jnp.sin(angles))


def local_any(signal, cotangent, band_freq, w_embed, b_embed, w_out, decay):
    devices = lax.axis_size("seq")
    rank_seq = lax.axis_index("seq")
    seg_len = signal.shape[1] * 2
    channels = signal.shape[2] // 2
    block_w = seg_len // devices
    rows_all = 2 * devices
    seq_total = seg_len * devices
    fft_size = 2 * seq_total
    inv_scale = 1.0 / fft_size
    radix_one = max(
        (divisor for divisor in range(1, math.isqrt(seg_len) + 1) if seg_len % divisor == 0)
    )
    radix_two = seg_len // radix_one
    row_ids = jnp.arange(rows_all, dtype=jnp.int32)
    src_ids = jnp.arange(devices, dtype=jnp.int32)
    col_glob = rank_seq * block_w + jnp.arange(block_w, dtype=jnp.int32)
    seg_ids = jnp.arange(seg_len, dtype=jnp.int32)
    one_ids = jnp.arange(radix_one, dtype=jnp.int32)
    two_ids = jnp.arange(radix_two, dtype=jnp.int32)
    pair_ids = lax.dynamic_slice_in_dim(row_ids, 2 * rank_seq, 2)
    outer_cos, outer_sin = angle_table(row_ids, src_ids, rows_all)
    entry_cos, entry_sin = angle_table(row_ids, col_glob, fft_size)
    first_cos, first_sin = angle_table(one_ids, one_ids, radix_one)
    second_cos, second_sin = angle_table(two_ids, two_ids, radix_two)
    inner_cos, inner_sin = angle_table(one_ids, two_ids, seg_len)
    exit_cos, exit_sin = angle_table(pair_ids, seg_ids, fft_size)
    inner_c = inner_cos[None, :, :, None]
    inner_s = inner_sin[None, :, :, None]

    def twist_stack(real_a, imag_a):
        real_a = real_a.reshape(rows_all, block_w, channels)
        imag_a = imag_a.reshape(rows_all, block_w, channels)
        twist_c = entry_cos[:, :, None]
        twist_s = entry_sin[:, :, None]
        real_b = real_a * twist_c + imag_a * twist_s
        imag_b = imag_a * twist_c - real_a * twist_s
        return jnp.stack([real_b, imag_b]).reshape(2, rows_all, block_w * channels)

    def column_pass(cols_data):
        return twist_stack(mat_dot(outer_cos, cols_data), -mat_dot(outer_sin, cols_data))

    def local_forward(stacked):
        grid = stacked.reshape(2, 2, radix_one, radix_two * channels)
        part_r = side_dot(first_cos, grid[0]) + side_dot(first_sin, grid[1])
        part_i = side_dot(first_cos, grid[1]) - side_dot(first_sin, grid[0])
        part_r = part_r.reshape(2, radix_one, radix_two, channels)
        part_i = part_i.reshape(2, radix_one, radix_two, channels)
        turn_r = part_r * inner_c + part_i * inner_s
        turn_i = part_i * inner_c - part_r * inner_s
        spec_r = inner_dot(second_cos, turn_r) + inner_dot(second_sin, turn_i)
        spec_i = inner_dot(second_cos, turn_i) - inner_dot(second_sin, turn_r)
        return (spec_r, spec_i)

    def local_inverse(spec_r, spec_i):
        back_r = inner_dot(second_cos, spec_r) - inner_dot(second_sin, spec_i)
        back_i = inner_dot(second_cos, spec_i) + inner_dot(second_sin, spec_r)
        turn_r = (back_r * inner_c - back_i * inner_s).reshape(2, radix_one, radix_two * channels)
        turn_i = (back_r * inner_s + back_i * inner_c).reshape(2, radix_one, radix_two * channels)
        time_r = (side_dot(first_cos, turn_r) - side_dot(first_sin, turn_i)).reshape(
            2, seg_len, channels
        )
        time_i = (side_dot(first_cos, turn_i) + side_dot(first_sin, turn_r)).reshape(
            2, seg_len, channels
        )
        twist_c = exit_cos[:, :, None]
        twist_s = exit_sin[:, :, None]
        final_r = time_r * twist_c - time_i * twist_s
        final_i = time_r * twist_s + time_i * twist_c
        return jnp.stack([final_r, final_i]).reshape(2, 2, seg_len * channels)

    def real_rows(gathered):
        return mat_dot(outer_cos.T, gathered[0]) - mat_dot(outer_sin.T, gathered[1])

    sig_cols, cot_cols = (
        lax.all_to_all(
            signal.reshape(devices, block_w * channels),
            "seq",
            split_axis=0,
            concat_axis=0,
            tiled=True,
        ),
        lax.all_to_all(
            cotangent.reshape(devices, block_w * channels),
            "seq",
            split_axis=0,
            concat_axis=0,
            tiled=True,
        ),
    )
    places = rank_seq * seg_len + seg_ids
    features, preact, hidden, taps, envelope = filter_parts(
        places, band_freq, w_embed, b_embed, w_out, decay, seq_total
    )
    tap_cols = lax.all_to_all(
        taps.reshape(devices, block_w * channels), "seq", split_axis=0, concat_axis=0, tiled=True
    )
    spec_sig, spec_cot, spec_tap = (
        lax.all_to_all(
            column_pass(sig_cols.astype(jnp.float32)),
            "seq",
            split_axis=1,
            concat_axis=2,
            tiled=True,
        ),
        lax.all_to_all(
            column_pass(cot_cols.astype(jnp.float32)),
            "seq",
            split_axis=1,
            concat_axis=2,
            tiled=True,
        ),
        lax.all_to_all(column_pass(tap_cols), "seq", split_axis=1, concat_axis=2, tiled=True),
    )
    sig_r, sig_i = local_forward(spec_sig)
    cot_r, cot_i = local_forward(spec_cot)
    tap_r, tap_i = local_forward(spec_tap)
    prod_r = sig_r * tap_r - sig_i * tap_i
    prod_i = sig_r * tap_i + sig_i * tap_r
    grad_r = cot_r * tap_r + cot_i * tap_i
    grad_i = cot_i * tap_r - cot_r * tap_i
    corr_r = cot_r * sig_r + cot_i * sig_i
    corr_i = cot_i * sig_r - cot_r * sig_i
    prod_back, grad_back, corr_back = (
        lax.all_to_all(
            local_inverse(prod_r, prod_i), "seq", split_axis=2, concat_axis=1, tiled=True
        ),
        lax.all_to_all(
            local_inverse(grad_r, grad_i), "seq", split_axis=2, concat_axis=1, tiled=True
        ),
        lax.all_to_all(
            local_inverse(corr_r, corr_i), "seq", split_axis=2, concat_axis=1, tiled=True
        ),
    )
    out_cols = real_rows(prod_back)
    dsig_cols = real_rows(grad_back)
    dtap_cols = real_rows(corr_back) * inv_scale
    out_rows, dsig_rows = (
        lax.all_to_all(
            (out_cols * inv_scale).astype(jnp.bfloat16),
            "seq",
            split_axis=0,
            concat_axis=0,
            tiled=True,
        ),
        lax.all_to_all(
            (dsig_cols * inv_scale).astype(jnp.bfloat16),
            "seq",
            split_axis=0,
            concat_axis=0,
            tiled=True,
        ),
    )
    conv_out = out_rows.reshape(1, seg_len // 2, 2 * channels)
    d_signal = dsig_rows.reshape(1, seg_len // 2, 2 * channels)
    d_taps = (
        lax.all_to_all(
            dtap_cols.astype(jnp.bfloat16), "seq", split_axis=0, concat_axis=0, tiled=True
        )
        .astype(dtap_cols.dtype)
        .reshape(seg_len, channels)
    )
    d_raw = d_taps * envelope
    d_preact = mat_dot(d_raw, w_out.T) * jnp.cos(preact)
    out_part = mat_dot(hidden.T, d_raw)
    embed_part = mat_dot(features.T, d_preact)
    bias_part = jnp.sum(d_preact, axis=0)
    out_sum, embed_sum, bias_sum = lax.psum((out_part, embed_part, bias_part), "seq")
    embed_all, bias_all = lax.psum((embed_sum, bias_sum), "chan")
    norm_scale = 1.0 / math.sqrt(seq_total)
    return (conv_out, d_signal, embed_all * norm_scale, bias_all * norm_scale, out_sum * norm_scale)


WIDE = 256
HALF = 128


def split_np(table):
    high = table.astype(jnp.bfloat16)
    low = (table - high.astype(np.float64)).astype(jnp.bfloat16)
    return np.stack([high, low])


def const_tables(devices, own, segs):
    blocks = devices * segs
    total = 2 * blocks * WIDE
    eye = np.eye(own)
    half_f = np.arange(blocks) + 0.5
    alpha = 2 * np.pi * half_f[:, None] * np.arange(blocks)[None, :] / (2 * blocks)
    outer = np.concatenate([np.kron(np.cos(alpha), eye), np.kron(-np.sin(alpha), eye)])
    lane = np.arange(WIDE)
    places = 2 * (lane % HALF) + lane // HALF
    theta = np.repeat(2 * np.pi * half_f[:, None] * places[None, :] / total, own, axis=0)
    twist = np.stack([np.cos(theta), np.sin(theta)]).astype(np.float32)
    phi = 2 * np.pi * (places[:, None] * np.arange(WIDE)[None, :] % WIDE) / WIDE
    inner = np.block([[np.cos(phi), -np.sin(phi)], [np.sin(phi), np.cos(phi)]])
    chans = devices * own
    pick = np.zeros((2, devices, segs, own, segs, 2, chans), np.float32)
    for h in range(2):
        for r in range(devices):
            for q in range(segs):
                for k in range(own):
                    pick[h, r, q, k, q, h, r * own + k] = 1.0
    pick = pick.reshape(2, devices * segs * own, segs * 2 * chans).astype(jnp.bfloat16)
    return split_np(outer), split_np(inner), twist, pick


def dot_nn(lhs, rhs):
    return lax.dot_general(lhs, rhs, (((1,), (0,)), ((), ())), preferred_element_type=jnp.float32)


def dot_nt(lhs, rhs):
    return lax.dot_general(lhs, rhs, (((1,), (1,)), ((), ())), preferred_element_type=jnp.float32)


def dot_tn(lhs, rhs):
    return lax.dot_general(lhs, rhs, (((0,), (0,)), ((), ())), preferred_element_type=jnp.float32)


def sin_cos(quarter):
    whole = jnp.round(quarter)
    rest = quarter - whole
    sq = rest * rest
    sin_p = rest * (1.5707963268 + sq * (-0.6459640975 + sq * (0.0796926262 + sq * (-0.0046817541 + sq * 0.00016044118))))
    cos_p = 1.0 + sq * (-1.2337005501 + sq * (0.2536695079 + sq * (-0.0208634807 + sq * (0.00091926027 - sq * 0.0000252020424))))
    turns = whole.astype(jnp.int32)
    odd = (turns & 1) == 1
    sin_v = jnp.where(odd, cos_p, sin_p)
    cos_v = jnp.where(odd, sin_p, cos_p)
    sin_v = jnp.where((turns & 2) == 2, -sin_v, sin_v)
    cos_v = jnp.where(((turns + 1) & 2) == 2, -cos_v, cos_v)
    return sin_v, cos_v


def fused_kernel(
    devices, planes, own, segs,
    freq_ref, sig_ref, cot_ref, pick_ref, outer_any, inner_any, twist_any,
    wemb_ref, bias_ref, wout_ref, decay_ref,
    conv_ref, dsig_ref, gemb_ref, gbias_ref, gcol_ref,
    send_a, recv_a, send_b, recv_b, send_e, recv_e, hid_ref, cos_ref, taps_ref, draw_ref,
    outer_ref, inner_ref, twist_ref, wmix_ref, rot_ref, tone_ref, wrow_ref, wcol_ref,
    gout_ref, gmix_ref, square_ref, send_c, recv_c, send_d, recv_d,
    send_sem, recv_sem, send_sem_d, recv_sem_d, load_sem,
):
    bf = jnp.bfloat16
    me = lax.axis_index("seq")
    blocks = devices * segs
    rows = blocks * own
    part = segs * own
    seq_total = blocks * WIDE
    per = WIDE // 64
    groups = blocks // per
    barrier = pltpu.get_barrier_semaphore()

    lane_id = lax.axis_index("chan")
    everyone = devices * planes
    mine = lane_id * devices + me

    def greet(step, carry):
        peer = lax.rem(mine + step, everyone)
        pl.semaphore_signal(
            barrier, inc=1,
            device_id={"seq": lax.rem(peer, devices), "chan": peer // devices},
            device_id_type=pl.DeviceIdType.MESH,
        )
        return carry

    lax.fori_loop(1, everyone, greet, 0)
    loads = [
        pltpu.make_async_copy(src, dst, load_sem.at[i])
        for i, (src, dst) in enumerate(
            [(outer_any, outer_ref), (inner_any, inner_ref), (twist_any, twist_ref)]
        )
    ]
    for load in loads:
        load.start()

    def copy_of(phase, src, dst, step):
        peer = lax.rem(me + step, devices)
        return pltpu.make_async_remote_copy(
            src_ref=src.at[peer],
            dst_ref=dst.at[me],
            send_sem=send_sem.at[phase, step],
            recv_sem=recv_sem.at[phase, step],
            device_id={"seq": peer},
            device_id_type=pl.DeviceIdType.MESH,
        )

    def start_all(phase, src, dst):
        def body(step, carry):
            copy_of(phase, src, dst, step).start()
            return carry

        lax.fori_loop(1, devices, body, 0)

    def wait_all(phase, src, dst):
        def body(step, carry):
            copy_of(phase, src, dst, step).wait()
            return carry

        lax.fori_loop(1, devices, body, 0)

    def pack(x_ref, at):
        wide = jnp.concatenate([x_ref[q * HALF:(q + 1) * HALF, :] for q in range(segs)], axis=1)
        mixed = jnp.concatenate([dot_nt(pick_ref[h], wide) for h in range(2)], axis=1)
        send_a[:, at:at + part, :] = mixed.astype(bf).reshape(devices, part, WIDE)

    pack(sig_ref, 0)
    pack(cot_ref, part)
    pl.semaphore_wait(barrier, everyone - 1)
    start_all(0, send_a, recv_a)
    recv_a[me] = send_a[me]

    turn_scale = 4.0 / seq_total
    far_lane = lax.broadcasted_iota(jnp.int32, (blocks, HALF), 1)
    far_row = lax.broadcasted_iota(jnp.int32, (blocks, HALF), 0)
    near_row = lax.broadcasted_iota(jnp.int32, (HALF, WIDE), 0)
    near_lane = lax.broadcasted_iota(jnp.int32, (HALF, WIDE), 1)
    lane_row = lax.broadcasted_iota(jnp.int32, (1, HALF), 1)
    lane_col = lax.broadcasted_iota(jnp.int32, (HALF, 1), 0)
    freq_row = jnp.zeros((1, HALF), jnp.int32)
    freq_col = jnp.zeros((HALF, 1), jnp.int32)
    for j in range(16):
        freq_row = jnp.where((lane_row & 15) == j, freq_ref[j], freq_row)
        freq_col = jnp.where((lane_col & 15) == j, freq_ref[j], freq_col)
    wrapped = (far_row * WIDE * freq_row) & (seq_total - 1)
    far_s, far_c = sin_cos(wrapped.astype(jnp.float32) * turn_scale)
    live = far_lane < 96
    rot_ref[0] = jnp.where(live, far_c, jnp.where(far_lane < 98, 1.0, 0.0))
    rot_ref[1] = jnp.where(live, jnp.where((far_lane & 16) == 0, far_s, -far_s), 0.0)
    spot = 2 * (near_lane & (HALF - 1)) + (near_lane >> 7)
    wrapped = (spot * freq_col) & (seq_total - 1)
    near_s, near_c = sin_cos(wrapped.astype(jnp.float32) * turn_scale)
    tone = jnp.where((near_row & 16) == 0, near_c, near_s)
    tone_hi = tone.astype(bf).astype(jnp.float32)
    tone = jnp.where((near_row >= 32) & (near_row < 64), tone - tone_hi, tone_hi)
    tone = jnp.where(near_row < 96, tone, jnp.where(near_row < 98, 1.0, 0.0))
    tone_ref[...] = tone.astype(bf)
    quarter_of = 2.0 / math.pi
    two_rows = lax.broadcasted_iota(jnp.int32, (8, 64), 0) < 2
    for side in range(2):
        square_ref[...] = jnp.zeros_like(square_ref)
        for rep in range(3):
            for half in range(2):
                at_row = rep * 32 + 16 * (half ^ side)
                square_ref[at_row:at_row + 16, 0:64] = wemb_ref[half * 16:half * 16 + 16, :] * quarter_of
        if side == 0:
            square_ref[96:104, 0:64] = jnp.where(two_rows, bias_ref[...] * quarter_of, 0.0)
        wmix_ref[side] = square_ref[...].T[0:64, :]
    per_own = per * own
    w_all = wout_ref[...]
    w_hi = w_all.astype(bf)
    w_lo = (w_all - w_hi.astype(jnp.float32)).astype(bf)
    chans = devices * own
    chan_at = lax.broadcasted_iota(jnp.int32, (per_own, chans), 1)
    chan_row = lax.broadcasted_iota(jnp.int32, (per_own, chans), 0)
    one_hot = jnp.where(chan_at == me * own + chan_row % own, 1.0, 0.0).astype(bf)
    row_keep = lax.broadcasted_iota(jnp.int32, (per_own, WIDE), 0) // own
    row_keep = row_keep == lax.broadcasted_iota(jnp.int32, (per_own, WIDE), 1) // 64
    col_keep = lax.broadcasted_iota(jnp.int32, (WIDE, per_own), 1) // own
    col_keep = col_keep == lax.broadcasted_iota(jnp.int32, (WIDE, per_own), 0) // 64
    for side, w_part in enumerate((w_hi, w_lo)):
        w_rep = jnp.concatenate([w_part] * per, axis=0)
        wrow_ref[side * per_own:(side + 1) * per_own, :] = jnp.where(
            row_keep, dot_nt(one_hot, w_rep), 0.0
        ).astype(bf)
        wcol_ref[side] = jnp.where(col_keep, dot_nt(w_rep, one_hot), 0.0).astype(bf)
    rate_at = lax.broadcasted_iota(jnp.int32, (rows, chans), 1)
    rate_row = lax.broadcasted_iota(jnp.int32, (rows, chans), 0)
    rate = jnp.sum(
        jnp.where(rate_at == me * own + rate_row % own, decay_ref[...], 0.0), axis=1, keepdims=True
    )
    peak = jnp.sqrt((1.0 + rate) / seq_total)

    lanes = lax.broadcasted_iota(jnp.int32, (64, HALF), 1)
    high_lane = (lanes < 64) | (lanes == 97)

    def net_step(g, carry):
        mixes = []
        for b in range(per):
            turn_c = rot_ref[0, pl.ds(g * per + b, 1), :]
            turn_s = rot_ref[1, pl.ds(g * per + b, 1), :]
            mix = wmix_ref[0] * turn_c + wmix_ref[1] * turn_s
            top = mix.astype(bf).astype(jnp.float32)
            mixes.append(jnp.where(high_lane, top, mix - top).astype(bf))
        quarter = dot_nn(jnp.concatenate(mixes, axis=0), tone_ref[...])
        sin_v, cos_v = sin_cos(quarter)
        hid = sin_v.astype(bf)
        at = pl.multiple_of(g * WIDE, WIDE)
        hid_ref[pl.ds(at, WIDE), :] = hid
        cos_ref[pl.ds(at, WIDE), :] = cos_v.astype(bf)
        both = dot_nn(wrow_ref[...], hid)
        taps_ref[pl.ds(pl.multiple_of(g * per * own, per * own), per * own), :] = (
            both[:per * own] + both[per * own:]
        )
        return carry

    lax.fori_loop(0, groups, net_step, 0, unroll=4)
    row_at = lax.broadcasted_iota(jnp.int32, (rows, WIDE), 0) // own
    lane_at = lax.broadcasted_iota(jnp.int32, (rows, WIDE), 1)
    fraction = (row_at * WIDE + 2 * (lane_at % HALF) + lane_at // HALF).astype(jnp.float32) / seq_total
    envelope = jnp.exp(-rate * fraction) * peak
    taps = taps_ref[...] * envelope

    for load in loads:
        load.wait()
    cos_t = twist_ref[0]
    sin_t = twist_ref[1]

    def rest_of(stage_r, stage_i):
        return jnp.concatenate(
            [stage_r * cos_t + stage_i * sin_t, stage_i * cos_t - stage_r * sin_t], axis=1
        ).astype(bf)

    def inner_fwd(turned):
        spec = dot_nn(turned, inner_ref[0]) + dot_nn(turned, inner_ref[1])
        return spec[:, :WIDE], spec[:, WIDE:]

    tap_hi = taps.astype(bf)
    tap_lo = (taps - tap_hi.astype(jnp.float32)).astype(bf)
    st = dot_nn(outer_ref[0], tap_hi) + dot_nn(outer_ref[1], tap_hi) + dot_nn(outer_ref[0], tap_lo)
    tap_r, tap_i = inner_fwd(rest_of(st[:rows], st[rows:]))

    wait_all(0, send_a, recv_a)

    def fwd(at):
        x = recv_a[:, at:at + part, :].reshape(rows, WIDE)
        stage = dot_nn(outer_ref[0], x) + dot_nn(outer_ref[1], x)
        return inner_fwd(rest_of(stage[:rows], stage[rows:]))

    sig_r, sig_i = fwd(0)
    cot_r, cot_i = fwd(part)

    def back(spec_r, spec_i):
        spec = jnp.concatenate([spec_r, spec_i], axis=1).astype(bf)
        time = dot_nt(spec, inner_ref[0]) + dot_nt(spec, inner_ref[1])
        time_r, time_i = time[:, :WIDE], time[:, WIDE:]
        turned = jnp.concatenate(
            [time_r * cos_t - time_i * sin_t, time_i * cos_t + time_r * sin_t], axis=0
        ).astype(bf)
        return (dot_tn(outer_ref[0], turned) + dot_tn(outer_ref[1], turned)) * (1.0 / seq_total)

    out = back(sig_r * tap_r - sig_i * tap_i, sig_r * tap_i + sig_i * tap_r)
    send_b[...] = out.astype(bf).reshape(devices, part, WIDE)
    start_all(1, send_b, recv_b)
    recv_b[me] = send_b[me]

    d_taps = back(cot_r * sig_r + cot_i * sig_i, cot_i * sig_r - cot_r * sig_i)
    draw_ref[...] = (d_taps * envelope).astype(bf)
    gout_ref[...] = jnp.zeros_like(gout_ref)
    gmix_ref[...] = jnp.zeros_like(gmix_ref)

    def grad_step(g, carry):
        at = pl.multiple_of(g * WIDE, WIDE)
        d_raw = draw_ref[pl.ds(pl.multiple_of(g * per * own, per * own), per * own), :]
        gout_ref[...] += dot_nt(d_raw, hid_ref[pl.ds(at, WIDE), :])
        d_hid = dot_nn(wcol_ref[0], d_raw) + dot_nn(wcol_ref[1], d_raw)
        d_pre = (d_hid * cos_ref[pl.ds(at, WIDE), :].astype(jnp.float32)).astype(bf)
        d_mix = dot_nt(d_pre, tone_ref[...])
        for b in range(per):
            turn_c = rot_ref[0, pl.ds(g * per + b, 1), :]
            turn_s = rot_ref[1, pl.ds(g * per + b, 1), :]
            piece = d_mix[b * 64:(b + 1) * 64, :]
            gmix_ref[0] += piece * turn_c
            gmix_ref[1] += piece * turn_s
        return carry

    lax.fori_loop(0, groups, grad_step, 0, unroll=4)

    mix_lane = lax.broadcasted_iota(jnp.int32, (64, HALF), 1)
    mix_s = gmix_ref[1]
    crossed = jnp.where(
        mix_lane < 16, pltpu.roll(mix_s, HALF - 16, 1),
        jnp.where(mix_lane < 32, pltpu.roll(mix_s, 16, 1), 0.0),
    )
    square_ref[0:64, :] = gmix_ref[0] + crossed
    keep = jnp.where(row_keep, gout_ref[...], 0.0)
    keep = keep[:, :HALF] + keep[:, HALF:]
    keep = keep + pltpu.roll(keep, 64, 1)
    square_ref[64:64 + per_own, :] = keep
    g_own = square_ref[64:64 + own, :]
    for b in range(1, per):
        g_own = g_own + square_ref[64 + b * own:64 + (b + 1) * own, :]
    for r in range(devices):
        send_c[r, 0:own, :] = square_ref[r * own:(r + 1) * own, :]
        send_c[r, own:2 * own, :] = g_own
    start_all(2, send_c, recv_c)
    recv_c[me] = send_c[me]
    out = back(cot_r * tap_r + cot_i * tap_i, cot_i * tap_r - cot_r * tap_i)
    send_e[...] = out.astype(bf).reshape(devices, part, WIDE)
    start_all(3, send_e, recv_e)
    recv_e[me] = send_e[me]
    wait_all(2, send_c, recv_c)
    summed = recv_c[0]
    for r in range(1, devices):
        summed = summed + recv_c[r]
    send_d[...] = summed

    def spread_of(step):
        peer = lax.rem(mine + step, everyone)
        return pltpu.make_async_remote_copy(
            src_ref=send_d,
            dst_ref=recv_d.at[mine],
            send_sem=send_sem_d.at[step],
            recv_sem=recv_sem_d.at[step],
            device_id={"seq": lax.rem(peer, devices), "chan": peer // devices},
            device_id_type=pl.DeviceIdType.MESH,
        )

    def spread_start(step, carry):
        spread_of(step).start()
        return carry

    def spread_wait(step, carry):
        spread_of(step).wait()
        return carry

    lax.fori_loop(1, everyone, spread_start, 0)
    recv_d[mine] = send_d[...]
    wait_all(1, send_b, recv_b)

    def unpack(o_ref, x_ref):
        x = x_ref[...].reshape(rows, WIDE)
        wide = dot_tn(x[:, :HALF], pick_ref[0]) + dot_tn(x[:, HALF:], pick_ref[1])
        for q in range(segs):
            o_ref[q * HALF:(q + 1) * HALF, :] = wide[:, q * HALF:(q + 1) * HALF].astype(bf)

    unpack(conv_ref, recv_b)
    wait_all(3, send_e, recv_e)
    unpack(dsig_ref, recv_e)
    lax.fori_loop(1, everyone, spread_wait, 0)
    for r in range(devices):
        total = recv_d[r]
        for other in range(1, planes):
            total = total + recv_d[other * devices + r]
        square_ref[r * own:(r + 1) * own, :] = total[0:own, :]
        square_ref[64 + r * own:64 + (r + 1) * own, :] = recv_c[r, own:2 * own, :]
    flipped = square_ref[...].T * (1.0 / math.sqrt(seq_total))
    gemb_ref[...] = flipped[0:32, 0:64]
    gbias_ref[...] = flipped[96:97, 0:64]
    gcol_ref[...] = flipped[0:64, 64:128]


def local(signal, cotangent, band_freq, w_embed, b_embed, w_out, decay):
    devices = lax.axis_size("seq")
    me = lax.axis_index("seq")
    seg_len = signal.shape[1] * 2
    chans = signal.shape[2] // 2
    own = chans // devices
    if (
        chans % devices or seg_len % WIDE or own != 4 or seg_len * devices & (seg_len * devices - 1)
        or seg_len * devices * 2048 > 2**30
        or w_embed.shape != (32, 64) or chans * 2 != HALF
    ):
        return local_any(signal, cotangent, band_freq, w_embed, b_embed, w_out, decay)
    segs = seg_len // WIDE
    blocks = devices * segs
    rows = blocks * own
    seq_total = seg_len * devices
    bf, f32 = jnp.bfloat16, jnp.float32
    hidden = 64
    per = WIDE // hidden
    planes = lax.axis_size("chan")
    outer, inner, twist, pick = const_tables(devices, own, segs)
    part = segs * own
    vmem = pl.BlockSpec(memory_space=pltpu.VMEM)
    away = pl.BlockSpec(memory_space=pl.ANY)
    conv, dsig, g_emb, g_bias, g_out = pl.pallas_call(
        functools.partial(fused_kernel, devices, planes, own, segs),
        out_shape=(
            jax.ShapeDtypeStruct(signal.shape[1:], bf),
            jax.ShapeDtypeStruct(signal.shape[1:], bf),
            jax.ShapeDtypeStruct((32, hidden), f32),
            jax.ShapeDtypeStruct((1, hidden), f32),
            jax.ShapeDtypeStruct((hidden, chans), f32),
        ),
        in_specs=[pl.BlockSpec(memory_space=pltpu.SMEM)] + [vmem] * 3 + [away] * 3 + [vmem] * 4,
        out_specs=(vmem,) * 5,
        scratch_shapes=[pltpu.VMEM((devices, 2 * part, WIDE), bf)] * 2
        + [pltpu.VMEM((devices, part, WIDE), bf)] * 4
        + [pltpu.VMEM((blocks * hidden, WIDE), bf)] * 2
        + [
            pltpu.VMEM((rows, WIDE), f32),
            pltpu.VMEM((rows, WIDE), bf),
            pltpu.VMEM(outer.shape, bf),
            pltpu.VMEM(inner.shape, bf),
            pltpu.VMEM(twist.shape, f32),
            pltpu.VMEM((2, hidden, HALF), f32),
            pltpu.VMEM((2, blocks, HALF), f32),
            pltpu.VMEM((HALF, WIDE), bf),
            pltpu.VMEM((2 * per * own, WIDE), bf),
            pltpu.VMEM((2, WIDE, per * own), bf),
            pltpu.VMEM((per * own, WIDE), f32),
            pltpu.VMEM((2, hidden, HALF), f32),
            pltpu.VMEM((HALF, HALF), f32),
            pltpu.VMEM((devices, 2 * own, HALF), f32),
            pltpu.VMEM((devices, 2 * own, HALF), f32),
            pltpu.VMEM((2 * own, HALF), f32),
            pltpu.VMEM((devices * planes, 2 * own, HALF), f32),
            pltpu.SemaphoreType.DMA((4, devices)),
            pltpu.SemaphoreType.DMA((4, devices)),
            pltpu.SemaphoreType.DMA((devices * planes,)),
            pltpu.SemaphoreType.DMA((devices * planes,)),
            pltpu.SemaphoreType.DMA((3,)),
        ],
        compiler_params=pltpu.CompilerParams(
            collective_id=0, has_side_effects=True, vmem_limit_bytes=56 * 2**20
        ),
    )(
        band_freq, signal[0], cotangent[0], jnp.asarray(pick), jnp.asarray(outer),
        jnp.asarray(inner), jnp.asarray(twist), w_embed, b_embed[None, :], w_out, decay[None, :],
    )
    return (conv[None], dsig[None], g_emb, g_bias[0], g_out)


def solution(mesh):
    return jax.shard_map(
        local,
        mesh=mesh,
        in_specs=(
            P("chan", "seq", None),
            P("chan", "seq", None),
            P(),
            P(),
            P(),
            P(None, "chan"),
            P("chan"),
        ),
        out_specs=(P("chan", "seq", None), P("chan", "seq", None), P(), P(), P(None, "chan")),
        check_vma=False,
    )
```
